128 devices in a mesh: tile: 16 (over x, z), dom: 8 (over y, core).
Axes of the slice: x: 4, y: 4, z: 4, core: 2. Of those that a mesh axis runs over, the one named last changes fastest.
Arguments:
- moisture: float32 [64, 128, 8192], P(None, 'dom', 'tile'), may hold values from -6 to 6
- ancestors: int32 [128], replicated, may hold values from 0 to 127, as said below
- adjacency: int32 [64, 3], replicated, may hold values from 0 to 63, as said below
- conductance: float32 [64, 3, 128, 128], P('tile'), may hold values from -0.15625 to 0.15625
- vertical: float32 [63, 8192], P(None, 'tile'), may hold values from 0.05 to 60
- rainfall: float32 [128, 8192], P('dom', 'tile'), may hold values from -6 to 6
Outputs:
- forecast: float32 [64, 128, 8192], P(None, 'dom', 'tile')
The draws below stay inside these ranges and needn't reach their ends.
Inputs may be any that keep to these rules, and one draw needn't show every extreme that they name: `ancestors`: each group of 16 new particles p with the same p // 16 copies at most 2 distinct old particles of any one group of 16 old particles, and exactly 2 distinct ones of the old group with the same index. `adjacency`: row b is b, then b or b - 1, then b or b + 1; b - 1 is named at blocks 64 // 2 and 28, b + 1 at blocks 64 // 2 - 1 and 35.
All inputs are finite; a program needn't handle non-finite values.
Results may differ from the reference program's by a relative error of at most 0.0003.
Values sent between devices are 32-bit elements; how exact they have to be, the bound alone decides.
No kernel may reach another device: no remote copies, remote signals or barrier semaphores. Data moves between devices by JAX's collectives and lax.ppermute only.
A program may use at most 192 MiB of HBM per device.

```python
import jax
import jax.numpy as jnp
from jax import lax

LAYERS = 64
BLOCK_COLS = 128
LINKS = 3
SUBSTEPS = 8
TILE_BLOCKS = 4
GROUP = 16
BLOCKS = 64
COLUMNS = 8192
PARTICLES = 128
CAP = 2
N_DOM = 8


def draw_ancestors(key, part):
    base = jax.random.fold_in(key, 17)
    key_a, key_b, key_c, key_d = jax.random.split(base, 4)
    diagonal = jnp.eye(N_DOM, dtype=bool)
    counts = jnp.where(diagonal, CAP, jax.random.randint(key_a, (N_DOM, N_DOM), 1, CAP + 1))
    scores = jax.random.randint(key_b, (N_DOM, N_DOM, GROUP), 0, 1 << 20) * GROUP + jnp.arange(GROUP, dtype=jnp.int32)
    order = jnp.argsort(scores, axis=-1).astype(jnp.int32)
    ends = jnp.cumsum(counts, axis=1)
    totals = ends[:, -1]
    picks = jax.random.randint(key_c, (N_DOM, GROUP), 0, totals[:, None])
    source = jnp.sum((picks[:, :, None] >= ends[:, None, :]).astype(jnp.int32), axis=2)
    starts = ends - counts
    slot = picks - jnp.take_along_axis(starts, source, axis=1)
    owner = jnp.arange(N_DOM, dtype=jnp.int32)[:, None] + jnp.zeros((N_DOM, GROUP), jnp.int32)
    leading = jnp.arange(GROUP, dtype=jnp.int32)[None, :] + jnp.zeros((N_DOM, GROUP), jnp.int32)
    early = leading < CAP
    source = jnp.where(early, owner, source)
    slot = jnp.where(early, leading, slot)
    local = jnp.take_along_axis(order.reshape(N_DOM, N_DOM * GROUP), source * GROUP + slot, axis=1)
    chosen = source * GROUP + local
    mixing = jax.random.randint(key_d, (N_DOM, GROUP), 0, 1 << 20) * GROUP + jnp.arange(GROUP, dtype=jnp.int32)
    shuffle = jnp.argsort(mixing, axis=1)
    chosen = jnp.take_along_axis(chosen, shuffle, axis=1)
    return chosen.reshape(-1).astype(jnp.int32)


def draw_adjacency(key, part):
    base = jax.random.fold_in(key, 29)
    offsets = jax.random.randint(base, (BLOCKS, 2), 0, 2)
    offsets = offsets.at[BLOCKS // 2, 0].set(1)
    offsets = offsets.at[BLOCKS // 2 - TILE_BLOCKS, 0].set(1)
    offsets = offsets.at[BLOCKS // 2 - 1, 1].set(1)
    offsets = offsets.at[BLOCKS // 2 + TILE_BLOCKS - 1, 1].set(1)
    blocks = jnp.arange(BLOCKS, dtype=jnp.int32)
    before = jnp.maximum(blocks - offsets[:, 0], 0)
    after = jnp.minimum(blocks + offsets[:, 1], BLOCKS - 1)
    return jnp.stack([blocks, before, after], axis=1).astype(jnp.int32)


def draw_vertical(key, part):
    base = jax.random.fold_in(key, 41)
    key_a, key_b, key_c, key_d = jax.random.split(base, 4)
    shape = (LAYERS - 1, COLUMNS)
    first = jax.random.uniform(key_a, shape, jnp.float32)
    second = jax.random.uniform(key_b, shape, jnp.float32)
    forced = jax.random.randint(key_d, (), 0, BLOCKS)
    block_ids = jnp.arange(BLOCKS, dtype=jnp.int32)
    weak = 0.05 * jnp.exp(jnp.log(100.0) * first)
    strong = 20.0 + 40.0 * second
    flags = jax.random.randint(key_c, (BLOCKS,), 0, 4) == 0
    flags = flags | (block_ids == forced)
    columns = jnp.repeat(flags, BLOCK_COLS, total_repeat_length=COLUMNS)
    values = jnp.where(columns[None, :], strong, weak)
    return values.astype(jnp.float32)


def block_levels(own_key, shape, pieces, least, high):
    loudness, own = 1.0, jax.random.fold_in(own_key, 6)
    for axis_at, shards_of in pieces:
        steps = jnp.exp(jax.random.uniform(jax.random.fold_in(own, axis_at), (shards_of,), jnp.float32, least / len(pieces), high / len(pieces)))
        loudness = loudness * jnp.repeat(steps, shape[axis_at] // shards_of).reshape([-1 if axis == axis_at else 1 for axis in range(len(shape))])
    return loudness


def noise(stream_key, dims, deviation, limit, shards=(), kind=jnp.bfloat16):
    gain = block_levels(stream_key, dims, shards, -0.22, 0.18) if shards else 1.0
    values = jax.random.normal(stream_key, dims, jnp.float32) * deviation * gain
    return jnp.minimum(jnp.maximum(values, -limit), limit).astype(kind)


def setup_inputs(seed: int = 0) -> dict:
    keys = jax.random.split(jax.random.key(seed), 7)
    return {
        "moisture": noise(keys[0], (LAYERS, PARTICLES, COLUMNS), 1.0, 6.0, ((1, 8), (2, 16)), jnp.float32),
        "ancestors": draw_ancestors(jax.random.fold_in(keys[6], 71), 0),
        "adjacency": draw_adjacency(jax.random.fold_in(keys[6], 71), 0),
        "conductance": noise(keys[3], (BLOCKS, LINKS, BLOCK_COLS, BLOCK_COLS), (4 * BLOCK_COLS * LINKS) ** -0.5, 0.15625, ((0, 16),), jnp.float32),
        "vertical": draw_vertical(jax.random.fold_in(keys[6], 71), 0),
        "rainfall": noise(keys[5], (PARTICLES, COLUMNS), 1.0, 6.0, ((0, 8), (1, 16)), jnp.float32),
    }


def factorize(vertical):
    zero = jnp.zeros_like(vertical[:1])
    above = jnp.concatenate([zero, vertical], 0)
    below = jnp.concatenate([vertical, zero], 0)
    diag = 1.0 + above + below

    def forward(e_prev, rows):
        d_row, a_row, b_row = rows
        inv = 1.0 / (d_row - a_row * e_prev)
        return b_row * inv, (inv, b_row * inv)

    _, (inverse, ecoef) = lax.scan(forward, jnp.zeros_like(vertical[0]), (diag, above, below))
    return above, inverse, ecoef


def solve(rhs, above, inverse, ecoef):
    def down(y_prev, rows):
        r_row, a_row, i_row = rows
        y_row = (r_row + a_row[None] * y_prev) * i_row[None]
        return y_row, y_row

    _, ys = lax.scan(down, jnp.zeros_like(rhs[0]), (rhs, above, inverse))

    def back(x_next, rows):
        y_row, e_row = rows
        x_row = y_row + e_row[None] * x_next
        return x_row, x_row

    _, xs = lax.scan(back, jnp.zeros_like(rhs[0]), (ys, ecoef), reverse=True)
    return xs


def reference(moisture, ancestors, adjacency, conductance, vertical, rainfall):
    state = jnp.take(moisture, ancestors.astype(jnp.int32), axis=1)
    above, inverse, ecoef = factorize(vertical)
    layers, count, width = state.shape
    nblk, nlink, span, _ = conductance.shape
    for step in range(SUBSTEPS):
        blocks = state.reshape(layers, count, nblk, span)
        flux = jnp.zeros_like(blocks)
        for link in range(nlink):
            picked = jnp.take(blocks, adjacency[:, link].astype(jnp.int32), axis=2)
            flux = flux + jnp.einsum("lpbc,bdc->lpbd", picked, conductance[:, link], precision=lax.Precision.HIGHEST)
        rhs = state + flux.reshape(layers, count, width)
        rhs = rhs.at[0].add(rainfall)
        state = solve(rhs, above, inverse, ecoef)
    return state
```

```python
import jax
import jax.numpy as jnp
from jax import lax
from jax.experimental import pallas as pl
from jax.experimental.pallas import tpu as pltpu
from jax.sharding import PartitionSpec as P

SUBSTEPS = 8
RING = 4
OWN = 4
LAYERS = 64
HALF = 32
SPAN = 128
WIDTH = 512
GROUP = 16
GROUPS = 8
PAIRS = 16
ROWS = HALF * 8
MSG = 2 * (3 * SPAN + LAYERS)
F32 = jnp.float32
BF16 = jnp.bfloat16
VMEM_LIMIT = 60 * 1024 * 1024


def params():
    return pltpu.CompilerParams(vmem_limit_bytes=VMEM_LIMIT)


def shape(dims, dtype=F32):
    return jax.ShapeDtypeStruct(dims, dtype)


SMEM = pl.BlockSpec(memory_space=pltpu.SMEM)
VMEM = pl.BlockSpec(memory_space=pltpu.VMEM)
ANY = pl.BlockSpec(memory_space=pl.ANY)


def z_pairs(s):
    return [(4 * x + z, 4 * x + (z + s) % 4) for x in range(4) for z in range(4)]


def x_pairs(s):
    out = []
    for x in range(4):
        for z in range(4):
            step = -1 if (z - s) % 4 < 2 else 1
            out.append((4 * x + z, 4 * ((x + step) % 4) + z))
    return out


def dom_pairs(r):
    return [(g, (g + r) % GROUPS) for g in range(GROUPS)]


def core_pairs():
    return [(g, g ^ 1) for g in range(GROUPS)]


def send_kernel(ids, anc, moist, *refs):
    outs, held, sems = refs[:GROUPS], refs[GROUPS], refs[GROUPS + 1]
    copies = []
    for t in range(WIDTH // SPAN):
        copies.append(pltpu.make_async_copy(moist.at[:, pl.ds(t * SPAN, SPAN)], held.at[t], sems.at[t]))
        copies[-1].start()
    for c in copies:
        c.wait()
    mine = ids[1]
    flip = 7 - lax.broadcasted_iota(jnp.int32, (8, SPAN), 0)
    for r in range(GROUPS):
        target = lax.rem(mine + r, GROUPS)
        low = jnp.int32(GROUP)
        high = jnp.int32(-1)
        for i in range(GROUP):
            v = anc[target * GROUP + i] - mine * GROUP
            inside = (v >= 0) & (v < GROUP)
            low = jnp.where(inside, jnp.minimum(low, v), low)
            high = jnp.where(inside, jnp.maximum(high, v), high)
        low = jnp.minimum(low, GROUP - 1)
        high = jnp.maximum(high, 0)
        for j, p in enumerate((low, high)):
            for t in range(WIDTH // SPAN):
                lanes = slice(t * SPAN, (t + 1) * SPAN)
                rows = held[t, pl.ds(p, LAYERS, stride=GROUP), :]
                outs[r][j, :HALF, lanes] = rows[:HALF]
                for q in range(HALF // 8):
                    part = rows[LAYERS - 8 * (q + 1):LAYERS - 8 * q]
                    outs[r][j, HALF + 8 * q:HALF + 8 * (q + 1), lanes] = jnp.take_along_axis(part, flip, axis=0)


def pack_kernel(ids, anc, rain, *refs):
    ins, outs = refs[:GROUPS], refs[GROUPS:GROUPS + RING]
    slots, least, sems = refs[GROUPS + RING:]
    copies = [pltpu.make_async_copy(ins[r], slots.at[pl.ds(2 * r, 2)], sems.at[r]) for r in range(GROUPS)]
    for c in copies:
        c.start()
    z = lax.rem(ids[0], RING)
    mine = ids[1]
    for g in range(GROUPS):
        least[g] = jnp.int32(1 << 20)
    for i in range(GROUP):
        v = anc[mine * GROUP + i]
        g = v // GROUP
        least[g] = jnp.minimum(least[g], v)
    for c in copies:
        c.wait()
    upper = lax.broadcasted_iota(jnp.int32, (8, WIDTH), 0) < 4
    for s in range(RING):
        owner = lax.rem(z + s, RING)
        for p in range(OWN):
            n = owner * OWN + p
            v = anc[mine * GROUP + n]
            g = v // GROUP
            slot = 2 * lax.rem(mine - g + GROUPS, GROUPS) + jnp.where(v > least[g], 1, 0)
            for t in range(WIDTH // SPAN):
                lanes = slice(t * SPAN, (t + 1) * SPAN)
                for d in range(2):
                    outs[s][t, pl.ds(4 * d + p, HALF, stride=8), :] = slots[slot, d * HALF:(d + 1) * HALF, lanes]
        own_rain = rain[pl.ds(pl.multiple_of(owner // 2 * 8, 8), 8), :]
        own_rain = jnp.where(lax.rem(owner, 2) == 1, pltpu.roll(own_rain, 4, 0), own_rain)
        own_rain = jnp.where(upper, own_rain, 0.0)
        for t in range(WIDTH // SPAN):
            outs[s][t, ROWS:, :] = own_rain[:, t * SPAN:(t + 1) * SPAN]


def coeff_kernel(ids, adj, cond, vert, out):
    tile = ids[0]
    core = lax.rem(ids[1], 2)
    eye = (lax.broadcasted_iota(jnp.int32, (SPAN, SPAN), 0) == lax.broadcasted_iota(jnp.int32, (SPAN, SPAN), 1)).astype(F32)
    for i in range(2):
        local = 2 * core + i
        b = RING * tile + local
        prev = jnp.where(adj[b, 1] == b, 0.0, 1.0).astype(F32)
        after = jnp.where(adj[b, 2] == b, 0.0, 1.0).astype(F32)
        own, first, second = cond[local, 0], cond[local, 1], cond[local, 2]
        base = i * (3 * SPAN + LAYERS)
        out[base:base + SPAN, :] = (first * prev).T
        out[base + SPAN:base + 2 * SPAN, :] = (own + first * (1.0 - prev) + second * (1.0 - after)).T + eye
        out[base + 2 * SPAN:base + 3 * SPAN, :] = (second * after).T
        lanes = pl.ds(pl.multiple_of(local * SPAN, SPAN), SPAN)
        out[base + 3 * SPAN:base + 3 * SPAN + LAYERS - 1, :] = vert[:, lanes]
        out[base + 3 * SPAN + LAYERS - 1:base + 3 * SPAN + LAYERS, :] = jnp.zeros((1, SPAN), F32)


def window_base(z, s, halo):
    t = lax.rem(z - s + RING, RING)
    if halo:
        return jnp.where(t < 2, 24 + 4 * t, 4 * t - 8)
    return 8 + 4 * t


def expand_kernel(ids, *refs):
    msgs = refs[:16]
    w_hi, w_lo, inv_ref, ai_ref, e_ref, d_ref = refs[16:22]
    vs = refs[22]
    z = lax.rem(ids[0], RING)
    core = lax.rem(ids[1], 2)
    zero = jnp.zeros((SPAN, SPAN), BF16)
    at = 0
    for halo in (False, True):
        for s in range(RING):
            base = window_base(z, s, halo) // 2
            for other in (0, 1):
                msg = msgs[at]
                at += 1
                half = core if other == 0 else 1 - core
                k = base + half
                for i in range(2):
                    row = i * (3 * SPAN + LAYERS)
                    cols = slice(i * SPAN, (i + 1) * SPAN)
                    for j in range(3):
                        w = msg[row + j * SPAN:row + (j + 1) * SPAN, :]
                        hi = w.astype(BF16)
                        lo = (w - hi.astype(F32)).astype(BF16)
                        rows = slice((i + j) * SPAN, (i + j + 1) * SPAN)
                        w_hi[k, rows, cols] = hi
                        w_lo[k, rows, cols] = lo
                    empty = slice(3 * SPAN, 4 * SPAN) if i == 0 else slice(0, SPAN)
                    w_hi[k, empty, cols] = zero
                    w_lo[k, empty, cols] = zero
                    vs[k, :, cols] = msg[row + 3 * SPAN:row + 3 * SPAN + LAYERS, :]
    upper = lax.broadcasted_iota(jnp.int32, (8, 2 * SPAN), 0) < 4
    group = 4

    def chunk(c, _):
        e_prev = [jnp.zeros((8, 2 * SPAN), F32)] * group
        for l in range(HALF):
            for q in range(group):
                k = c * group + q
                a_low = vs[k, LAYERS - 1 - l:LAYERS - l, :]
                a_top = vs[k, l - 1:l, :] if l else jnp.zeros((1, 2 * SPAN), F32)
                a = jnp.where(upper, a_top, a_low)
                b = jnp.where(upper, vs[k, l:l + 1, :], vs[k, LAYERS - 2 - l:LAYERS - 1 - l, :])
                inv = 1.0 / (1.0 + a + b - a * e_prev[q])
                e = b * inv
                inv_ref[k, l] = inv
                ai_ref[k, l] = a * inv
                e_ref[k, l] = e
                e_prev[q] = e
        for q in range(group):
            e = e_prev[q]
            d_ref[c * group + q] = 1.0 / (1.0 - e * pltpu.roll(e, 4, 0))
        return 0

    lax.fori_loop(0, PAIRS // group, chunk, 0)


def step_kernel(ids, *refs):
    ins = refs[:8]
    w_hi, w_lo, inv_ref, ai_ref, e_ref, d_ref = refs[8:14]
    outs = refs[14:18]
    xh0, xl0, xh1, xl1, rain, r_a, r_b, final, sems = refs[18:]
    z = lax.rem(ids[0], RING)
    pad = jnp.zeros((ROWS, SPAN), BF16)
    for ref in (xh0, xl0):
        ref[:, :SPAN] = pad
        ref[:, (2 * PAIRS + 1) * SPAN:] = pad
    at = 0
    for halo in (False, True):
        for s in range(RING):
            src = ins[at]
            at += 1
            base = window_base(z, s, halo)
            for t in range(WIDTH // SPAN):
                lanes = pl.ds(pl.multiple_of((base + 1 + t) * SPAN, SPAN), SPAN)
                v = src[t, :ROWS, :]
                hi = v.astype(BF16)
                xh0[:, lanes] = hi
                xl0[:, lanes] = (v - hi.astype(F32)).astype(BF16)
                rain[:, pl.ds(pl.multiple_of((base + t) * SPAN, SPAN), SPAN)] = src[t, ROWS:, :]

    def product(k, xh, xl, r):
        lanes = pl.ds(pl.multiple_of(k * 2 * SPAN, 2 * SPAN), 4 * SPAN)
        h = xh[:, lanes]
        w = w_hi[k]
        acc = jnp.dot(h, w, preferred_element_type=F32)
        acc = acc + jnp.dot(xl[:, lanes], w, preferred_element_type=F32)
        acc = acc + jnp.dot(h, w_lo[k], preferred_element_type=F32)
        r[...] = acc
        r[:8, :] = acc[:8, :] + rain[:, pl.ds(pl.multiple_of(k * 2 * SPAN, 2 * SPAN), 2 * SPAN)]

    def solve(k, r, put):
        y = r[:8, :] * inv_ref[k, 0]
        r[:8, :] = y
        for l in range(1, HALF):
            y = r[8 * l:8 * l + 8, :] * inv_ref[k, l] + ai_ref[k, l] * y
            if l < HALF - 1:
                r[8 * l:8 * l + 8, :] = y
        x = (y + e_ref[k, HALF - 1] * pltpu.roll(y, 4, 0)) * d_ref[k]
        later = x
        for l in range(HALF - 2, -1, -1):
            x = r[8 * l:8 * l + 8, :] + e_ref[k, l] * x
            if l % 2:
                later = x
            else:
                put(k, l // 2, jnp.concatenate([x, later], axis=0))

    for step in range(1, SUBSTEPS + 1):
        src = (xh0, xl0) if step % 2 else (xh1, xl1)
        dst = (xh1, xl1) if step % 2 else (xh0, xl0)
        first, last = step // 2, PAIRS - step // 2

        def put(k, m, v, dst=dst):
            lanes = pl.ds(pl.multiple_of((2 * k + 1) * SPAN, SPAN), 2 * SPAN)
            hi = v.astype(BF16)
            dst[0][16 * m:16 * m + 16, lanes] = hi
            dst[1][16 * m:16 * m + 16, lanes] = (v - hi.astype(F32)).astype(BF16)

        def put_final(k, m, v):
            t = (k - 4) // 2
            s = lax.rem(t - z + RING, RING)
            lanes = pl.ds(pl.multiple_of(lax.rem(k, 2) * 2 * SPAN, 2 * SPAN), 2 * SPAN)
            final[s, 16 * m:16 * m + 16, lanes] = v

        write = put_final if step == SUBSTEPS else put

        product(first, *src, r_a)

        def body(i, _, first=first, src=src, write=write):
            k = first + 2 * i
            product(k + 1, *src, r_b)
            solve(k, r_a, write)
            product(k + 2, *src, r_a)
            solve(k + 1, r_b, write)
            return 0

        lax.fori_loop(0, (last - first) // 2 - 1, body, 0)
        product(last - 1, *src, r_b)
        solve(last - 2, r_a, write)
        solve(last - 1, r_b, write)

    copies = [pltpu.make_async_copy(final.at[s], outs[s], sems.at[s]) for s in range(RING)]
    for c in copies:
        c.start()
    for c in copies:
        c.wait()


def join_kernel(ids, *refs):
    ins, out, held, sems = refs[:RING], refs[RING], refs[RING + 1], refs[RING + 2]
    z = lax.rem(ids[0], RING)
    copies = []
    for s in range(RING):
        copies.append(pltpu.make_async_copy(ins[s], held.at[lax.rem(z - s + RING, RING)], sems.at[s]))
        copies[-1].start()
    for c in copies:
        c.wait()
    upper = lax.broadcasted_iota(jnp.int32, (8, WIDTH), 0) < 4

    def body(l, _):
        rows = pl.ds(pl.multiple_of(l * 8, 8), 8)
        for h in range(2):
            a = held[2 * h, rows, :]
            b = held[2 * h + 1, rows, :]
            out[l, 8 * h:8 * h + 8, :] = jnp.where(upper, a, pltpu.roll(b, 4, 0))
            out[LAYERS - 1 - l, 8 * h:8 * h + 8, :] = jnp.where(upper, pltpu.roll(a, 4, 0), b)
        return 0

    lax.fori_loop(0, HALF, body, 0, unroll=4)


def shards(moisture, ancestors, adjacency, conductance, vertical, rainfall):
    ids = jnp.stack([lax.axis_index("tile"), lax.axis_index("dom")]).astype(jnp.int32)

    flat = moisture.reshape(LAYERS * GROUP, WIDTH)
    sent = pl.pallas_call(
        send_kernel,
        out_shape=[shape((2, LAYERS, WIDTH))] * GROUPS,
        in_specs=[SMEM, SMEM, ANY],
        out_specs=[VMEM] * GROUPS,
        scratch_shapes=[
            pltpu.VMEM((WIDTH // SPAN, LAYERS * GROUP, SPAN), F32),
            pltpu.SemaphoreType.DMA((WIDTH // SPAN,)),
        ],
        compiler_params=params(),
    )(ids, ancestors, flat)
    coeff = pl.pallas_call(
        coeff_kernel,
        out_shape=shape((MSG, SPAN)),
        in_specs=[SMEM, SMEM, VMEM, VMEM],
        out_specs=VMEM,
        compiler_params=params(),
    )(ids, adjacency, conductance, vertical)

    got = [sent[0]] + [lax.ppermute(sent[r], "dom", dom_pairs(r)) for r in range(1, GROUPS)]
    c_ring = [coeff] + [lax.ppermute(coeff, "tile", z_pairs(s)) for s in range(1, RING)]
    c_side = [lax.ppermute(c_ring[s], "tile", x_pairs(s)) for s in range(RING)]
    c_all = []
    for c in c_ring + c_side:
        c_all += [c, lax.ppermute(c, "dom", core_pairs())]

    mine = pl.pallas_call(
        pack_kernel,
        out_shape=[shape((WIDTH // SPAN, ROWS + 8, SPAN))] * RING,
        in_specs=[SMEM, SMEM, VMEM] + [ANY] * GROUPS,
        out_specs=[VMEM] * RING,
        scratch_shapes=[
            pltpu.VMEM((2 * GROUPS, LAYERS, WIDTH), F32),
            pltpu.SMEM((GROUPS,), jnp.int32),
            pltpu.SemaphoreType.DMA((GROUPS,)),
        ],
        compiler_params=params(),
    )(ids, ancestors, rainfall, *got)
    ring = [mine[0]] + [lax.ppermute(mine[s], "tile", z_pairs(s)) for s in range(1, RING)]
    side = [lax.ppermute(ring[s], "tile", x_pairs(s)) for s in range(RING)]

    coefs = pl.pallas_call(
        expand_kernel,
        out_shape=[shape((PAIRS, 4 * SPAN, 2 * SPAN), BF16)] * 2
        + [shape((PAIRS, HALF, 8, 2 * SPAN))] * 3
        + [shape((PAIRS, 8, 2 * SPAN))],
        in_specs=[SMEM] + [VMEM] * 16,
        out_specs=[VMEM] * 6,
        scratch_shapes=[pltpu.VMEM((PAIRS, LAYERS, 2 * SPAN), F32)],
        compiler_params=params(),
    )(ids, *c_all)

    wide = (ROWS, (2 * PAIRS + 2) * SPAN)
    back = pl.pallas_call(
        step_kernel,
        out_shape=[shape((ROWS, WIDTH))] * RING,
        in_specs=[SMEM] + [VMEM] * 14,
        out_specs=[ANY] * RING,
        scratch_shapes=[pltpu.VMEM(wide, BF16)] * 4
        + [
            pltpu.VMEM((8, 2 * PAIRS * SPAN), F32),
            pltpu.VMEM((ROWS, 2 * SPAN), F32),
            pltpu.VMEM((ROWS, 2 * SPAN), F32),
            pltpu.VMEM((RING, ROWS, WIDTH), F32),
            pltpu.SemaphoreType.DMA((RING,)),
        ],
        compiler_params=params(),
    )(ids, *ring, *side, *coefs)

    home = [back[0]] + [lax.ppermute(back[s], "tile", z_pairs(s)) for s in range(1, RING)]
    return pl.pallas_call(
        join_kernel,
        out_shape=shape((LAYERS, GROUP, WIDTH)),
        in_specs=[SMEM] + [ANY] * RING,
        out_specs=VMEM,
        scratch_shapes=[pltpu.VMEM((RING, ROWS, WIDTH), F32), pltpu.SemaphoreType.DMA((RING,))],
        compiler_params=params(),
    )(ids, *home)


def solution(mesh):
    in_specs = (
        P(None, "dom", "tile"),
        P(),
        P(),
        P("tile", None, None, None),
        P(None, "tile"),
        P("dom", "tile"),
    )
    out_specs = P(None, "dom", "tile")
    return jax.shard_map(shards, mesh=mesh, in_specs=in_specs, out_specs=out_specs, check_vma=False)
```

```python
import jax
import jax.numpy as jnp
from jax import lax
from jax.experimental import pallas as pl
from jax.experimental.pallas import tpu as pltpu
from jax.sharding import PartitionSpec as P

SUBSTEPS = 8
RING = 4
OWN = 4
LAYERS = 64
HALF = 32
SPAN = 128
WIDTH = 512
GROUP = 16
GROUPS = 8
PAIRS = 16
ROWS = HALF * 8
MSG = 2 * (3 * SPAN + LAYERS)
F32 = jnp.float32
BF16 = jnp.bfloat16


def params(mib):
    return pltpu.CompilerParams(vmem_limit_bytes=mib * 1024 * 1024)


def shape(dims, dtype=F32):
    return jax.ShapeDtypeStruct(dims, dtype)


SMEM = pl.BlockSpec(memory_space=pltpu.SMEM)
VMEM = pl.BlockSpec(memory_space=pltpu.VMEM)
ANY = pl.BlockSpec(memory_space=pl.ANY)


def z_pairs(s):
    return [(4 * x + z, 4 * x + (z + s) % 4) for x in range(4) for z in range(4)]


def x_pairs(s):
    out = []
    for x in range(4):
        for z in range(4):
            step = -1 if (z - s) % 4 < 2 else 1
            out.append((4 * x + z, 4 * ((x + step) % 4) + z))
    return out


def core_pairs():
    return [(g, g ^ 1) for g in range(GROUPS)]


def send_kernel(ids, anc, moist, out, held, ready, sems, out_sems):
    copies = []
    for t in range(WIDTH // SPAN):
        copies.append(pltpu.make_async_copy(moist.at[:, pl.ds(t * SPAN, SPAN)], held.at[t], sems.at[t]))
        copies[-1].start()
    mine = ids[1]
    flip = 7 - lax.broadcasted_iota(jnp.int32, (8, SPAN), 0)
    picks = []
    for target in range(GROUPS):
        low = jnp.int32(GROUP)
        high = jnp.int32(-1)
        for i in range(GROUP):
            v = anc[target * GROUP + i] - mine * GROUP
            inside = (v >= 0) & (v < GROUP)
            low = jnp.where(inside, jnp.minimum(low, v), low)
            high = jnp.where(inside, jnp.maximum(high, v), high)
        picks.append((jnp.minimum(low, GROUP - 1), jnp.maximum(high, 0)))
    for c in copies:
        c.wait()
    leave = []
    for r in range(GROUPS):
        for j in range(2):
            for t in range(WIDTH // SPAN):
                lanes = slice(t * SPAN, (t + 1) * SPAN)
                rows = held[t, pl.ds(picks[r][j], LAYERS, stride=GROUP), :]
                ready[2 * r + j, :HALF, lanes] = rows[:HALF]
                for q in range(HALF // 8):
                    part = rows[LAYERS - 8 * (q + 1):LAYERS - 8 * q]
                    ready[2 * r + j, HALF + 8 * q:HALF + 8 * (q + 1), lanes] = jnp.take_along_axis(part, flip, axis=0)
        span = pl.ds(2 * r, 2)
        leave.append(pltpu.make_async_copy(ready.at[span], out.at[span], out_sems.at[r]))
        leave[-1].start()
    for c in leave:
        c.wait()


def pack_kernel(ids, anc, rain, *refs):
    arrived, outs = refs[0], refs[1:1 + RING]
    slots, ready, least, sem, out_sems = refs[1 + RING:]
    fetch = pltpu.make_async_copy(arrived, slots, sem)
    fetch.start()
    z = lax.rem(ids[0], RING)
    mine = ids[1]
    for g in range(GROUPS):
        least[g] = jnp.int32(1 << 20)
    for i in range(GROUP):
        v = anc[mine * GROUP + i]
        g = v // GROUP
        least[g] = jnp.minimum(least[g], v)
    fetch.wait()
    upper = lax.broadcasted_iota(jnp.int32, (8, WIDTH), 0) < 4
    leave = []
    for s in list(range(1, RING)) + [0]:
        owner = lax.rem(z + s, RING)
        for p in range(OWN):
            v = anc[mine * GROUP + owner * OWN + p]
            g = v // GROUP
            slot = 2 * g + jnp.where(v > least[g], 1, 0)
            for t in range(WIDTH // SPAN):
                lanes = slice(t * SPAN, (t + 1) * SPAN)
                for d in range(2):
                    ready[s, t, pl.ds(4 * d + p, HALF, stride=8), :] = slots[slot, d * HALF:(d + 1) * HALF, lanes]
        own_rain = rain[pl.ds(pl.multiple_of(owner // 2 * 8, 8), 8), :]
        own_rain = jnp.where(lax.rem(owner, 2) == 1, pltpu.roll(own_rain, 4, 0), own_rain)
        own_rain = jnp.where(upper, own_rain, 0.0)
        for t in range(WIDTH // SPAN):
            ready[s, t, ROWS:, :] = own_rain[:, t * SPAN:(t + 1) * SPAN]
        leave.append(pltpu.make_async_copy(ready.at[s], outs[s], out_sems.at[s]))
        leave[-1].start()
    for c in leave:
        c.wait()


def coeff_kernel(ids, adj, cond, vert, after, out):
    tile = ids[0]
    core = lax.rem(ids[1], 2)
    eye = (lax.broadcasted_iota(jnp.int32, (SPAN, SPAN), 0) == lax.broadcasted_iota(jnp.int32, (SPAN, SPAN), 1)).astype(F32)
    links = adj[...]
    block = lax.broadcasted_iota(jnp.int32, links.shape, 1)
    place = lax.broadcasted_iota(jnp.int32, links.shape, 0)
    other = jnp.where(links == block, 0.0, 1.0).astype(F32)
    for i in range(2):
        local = 2 * core + i
        b = RING * tile + local
        prev = jnp.sum(jnp.where((block == b) & (place == 1), other, 0.0))
        after = jnp.sum(jnp.where((block == b) & (place == 2), other, 0.0))
        own, first, second = cond[local, 0], cond[local, 1], cond[local, 2]
        base = i * (3 * SPAN + LAYERS)
        out[base:base + SPAN, :] = (first * prev).T
        out[base + SPAN:base + 2 * SPAN, :] = (own + first * (1.0 - prev) + second * (1.0 - after)).T + eye
        out[base + 2 * SPAN:base + 3 * SPAN, :] = (second * after).T
        lanes = pl.ds(pl.multiple_of(local * SPAN, SPAN), SPAN)
        out[base + 3 * SPAN:base + 3 * SPAN + LAYERS - 1, :] = vert[:, lanes]
        out[base + 3 * SPAN + LAYERS - 1:base + 3 * SPAN + LAYERS, :] = jnp.zeros((1, SPAN), F32)


def window_base(z, s, halo):
    t = lax.rem(z - s + RING, RING)
    if halo:
        return jnp.where(t < 2, 24 + 4 * t, 4 * t - 8)
    return 8 + 4 * t


def expand_kernel(ids, mine, other, w_ref, c_ref, vs):
    z = lax.rem(ids[0], RING)
    core = lax.rem(ids[1], 2)
    for at in range(2 * RING):
        base = window_base(z, at % RING, at >= RING) // 2
        for msg, half in ((mine, core), (other, 1 - core)):
            k = base + half
            for i in range(2):
                row = i * (3 * SPAN + LAYERS)
                cols = slice(i * SPAN, (i + 1) * SPAN)
                rows = slice(i * SPAN, (i + 3) * SPAN)
                w = msg[at, row:row + 3 * SPAN, :]
                hi = w.astype(BF16)
                w_ref[k, 0, rows, cols] = hi
                w_ref[k, 1, rows, cols] = (w - hi.astype(F32)).astype(BF16)
                empty = slice(3 * SPAN, 4 * SPAN) if i == 0 else slice(0, SPAN)
                w_ref[k, 0, empty, cols] = jnp.zeros((SPAN, SPAN), BF16)
                w_ref[k, 1, empty, cols] = jnp.zeros((SPAN, SPAN), BF16)
                vs[k, :, i * SPAN:(i + 1) * SPAN] = msg[at, row + 3 * SPAN:row + 3 * SPAN + LAYERS, :]
    first = lax.broadcasted_iota(jnp.int32, (2, 2 * SPAN), 0) == 0
    group = 8

    def chunk(c, _):
        e_prev = [jnp.zeros((2, 2 * SPAN), F32)] * group
        for l in range(HALF):
            for q in range(group):
                k = c * group + q
                a_low = vs[k, LAYERS - 1 - l:LAYERS - l, :]
                a_top = vs[k, l - 1:l, :] if l else jnp.zeros((1, 2 * SPAN), F32)
                a = jnp.where(first, a_top, a_low)
                b = jnp.where(first, vs[k, l:l + 1, :], vs[k, LAYERS - 2 - l:LAYERS - 1 - l, :])
                inv = 1.0 / (1.0 + a + b - a * e_prev[q])
                e = b * inv
                c_ref[k, 2 * l:2 * l + 2] = inv
                c_ref[k, 2 * (HALF + l):2 * (HALF + l) + 2] = a * inv
                c_ref[k, 2 * (2 * HALF + l):2 * (2 * HALF + l) + 2] = e
                e_prev[q] = e
        for q in range(group):
            e = e_prev[q]
            both = 1.0 / (1.0 - e[0:1] * e[1:2])
            c_ref[c * group + q, 6 * HALF:6 * HALF + 8] = jnp.broadcast_to(both, (8, 2 * SPAN))
        return 0

    lax.fori_loop(0, PAIRS // group, chunk, 0)


def step_kernel(ids, *refs):
    ins, w, packed, outs = refs[:8], refs[8], refs[9], refs[10:14]
    x0, x1, rain, r_a, r_b, r_c, r_d, final, c, sems = refs[14:]
    z = lax.rem(ids[0], RING)
    upper = lax.broadcasted_iota(jnp.int32, (8, 2 * SPAN), 0) < 4

    def spread(k):
        for l in range(3 * HALF):
            c[k, l] = jnp.where(upper, packed[k, 2 * l:2 * l + 1, :], packed[k, 2 * l + 1:2 * l + 2, :])
        c[k, 3 * HALF] = packed[k, 6 * HALF:6 * HALF + 8, :]

    pad = jnp.zeros((2 * ROWS, SPAN), BF16)
    x0[:, :SPAN] = pad
    x0[:, (2 * PAIRS + 1) * SPAN:] = pad
    at = 0
    for halo in (False, True):
        for s in range(RING):
            base = window_base(z, s, halo)
            for t in range(WIDTH // SPAN):
                lanes = pl.ds(pl.multiple_of((base + 1 + t) * SPAN, SPAN), SPAN)
                v = ins[at][t, :ROWS, :]
                hi = v.astype(BF16)
                x0[:ROWS, lanes] = hi
                x0[ROWS:, lanes] = (v - hi.astype(F32)).astype(BF16)
                rain[:, pl.ds(pl.multiple_of((base + t) * SPAN, SPAN), SPAN)] = ins[at][t, ROWS:, :]
            at += 1

    def product(k, x, r):
        lanes = pl.ds(pl.multiple_of(k * 2 * SPAN, 2 * SPAN), 4 * SPAN)
        both = jnp.dot(x[:, lanes], w[k, 0], preferred_element_type=F32)
        acc = jnp.dot(x[:ROWS, lanes], w[k, 1], preferred_element_type=F32)
        acc = both[:ROWS] + (both[ROWS:] + acc)
        r[...] = acc
        r[:8, :] = acc[:8, :] + rain[:, pl.ds(pl.multiple_of(k * 2 * SPAN, 2 * SPAN), 2 * SPAN)]

    def forward(k, rs):
        ys = [r[:8, :] * c[k + q, 0] for q, r in enumerate(rs)]
        for q, r in enumerate(rs):
            r[:8, :] = ys[q]
        for l in range(1, HALF):
            for q, r in enumerate(rs):
                ys[q] = r[8 * l:8 * l + 8, :] * c[k + q, l] + c[k + q, HALF + l] * ys[q]
                if l < HALF - 1:
                    r[8 * l:8 * l + 8, :] = ys[q]
        return ys

    def backward(k, rs, ys, put):
        xs = [(y + c[k + q, 3 * HALF - 1] * pltpu.roll(y, 4, 0)) * c[k + q, 3 * HALF] for q, y in enumerate(ys)]
        later = list(xs)
        for l in range(HALF - 2, -1, -1):
            for q, r in enumerate(rs):
                xs[q] = r[8 * l:8 * l + 8, :] + c[k + q, 2 * HALF + l] * xs[q]
                if l % 2:
                    later[q] = xs[q]
                else:
                    put(k + q, l // 2, jnp.concatenate([xs[q], later[q]], axis=0))

    for step in range(1, SUBSTEPS + 1):
        src, dst = (x0, x1) if step % 2 else (x1, x0)
        first, last = step // 2, PAIRS - step // 2
        groups = (last - first) // 2

        def put(k, m, v, dst=dst):
            lanes = pl.ds(pl.multiple_of((2 * k + 1) * SPAN, SPAN), 2 * SPAN)
            hi = v.astype(BF16)
            dst[16 * m:16 * m + 16, lanes] = hi
            dst[ROWS + 16 * m:ROWS + 16 * m + 16, lanes] = (v - hi.astype(F32)).astype(BF16)

        def put_final(k, m, v):
            t = (k - 4) // 2
            s = lax.rem(t - z + RING, RING)
            lanes = pl.ds(pl.multiple_of(lax.rem(k, 2) * 2 * SPAN, 2 * SPAN), 2 * SPAN)
            final[s, 16 * m:16 * m + 16, lanes] = v

        write = put_final if step == SUBSTEPS else put

        def one(k, r, src=src):
            product(k, src, r)

        def ready(k, n, step=step):
            if step == 1:
                for q in range(n):
                    spread(k + q)

        near, far = (r_a, r_b), (r_c, r_d)
        one(first, r_a)
        one(first + 1, r_b)

        def body(i, _, first=first, one=one, ready=ready, write=write):
            k = first + 4 * i
            for at, (old, new) in ((k, (near, far)), (k + 2, (far, near))):
                ready(at, 2)
                one(at + 2, new[0])
                ys = forward(at, old)
                one(at + 3, new[1])
                backward(at, old, ys, write)
            return 0

        lax.fori_loop(0, (groups - 1) // 2, body, 0)
        rest = [(last - 2, near)]
        if groups % 2 == 0:
            ready(last - 4, 2)
            one(last - 2, r_c)
            ys = forward(last - 4, near)
            one(last - 1, r_d)
            backward(last - 4, near, ys, write)
            rest = [(last - 2, far)]
        for at, old in rest:
            ready(at, 2)
            backward(at, old, forward(at, old), write)

    copies = [pltpu.make_async_copy(final.at[s], outs[s], sems.at[s]) for s in range(RING)]
    for c_out in copies:
        c_out.start()
    for c_out in copies:
        c_out.wait()


def join_kernel(ids, *refs):
    ins, out, held, ready, sems, out_sems = refs[:RING], *refs[RING:]
    z = lax.rem(ids[0], RING)
    copies = []
    for s in range(RING):
        copies.append(pltpu.make_async_copy(ins[s], held.at[lax.rem(z - s + RING, RING)], sems.at[s]))
        copies[-1].start()
    for c in copies:
        c.wait()
    upper = lax.broadcasted_iota(jnp.int32, (8, WIDTH), 0) < 4
    parts = 4
    depth = HALF // parts
    leave = []
    for part in range(parts):
        for l in range(part * depth, (part + 1) * depth):
            for h in range(2):
                a = held[2 * h, 8 * l:8 * l + 8, :]
                b = held[2 * h + 1, 8 * l:8 * l + 8, :]
                ready[l, 8 * h:8 * h + 8, :] = jnp.where(upper, a, pltpu.roll(b, 4, 0))
                ready[LAYERS - 1 - l, 8 * h:8 * h + 8, :] = jnp.where(upper, pltpu.roll(a, 4, 0), b)
        for i, low in enumerate((part * depth, LAYERS - (part + 1) * depth)):
            span = pl.ds(low, depth)
            leave.append(pltpu.make_async_copy(ready.at[span], out.at[span], out_sems.at[2 * part + i]))
            leave[-1].start()
    for c in leave:
        c.wait()


def shards(moisture, ancestors, adjacency, conductance, vertical, rainfall):
    ids = jnp.stack([lax.axis_index("tile"), lax.axis_index("dom")]).astype(jnp.int32)

    flat = moisture.reshape(LAYERS * GROUP, WIDTH)
    sent = pl.pallas_call(
        send_kernel,
        out_shape=shape((2 * GROUPS, LAYERS, WIDTH)),
        in_specs=[SMEM, SMEM, ANY],
        out_specs=ANY,
        scratch_shapes=[
            pltpu.VMEM((WIDTH // SPAN, LAYERS * GROUP, SPAN), F32),
            pltpu.VMEM((2 * GROUPS, LAYERS, WIDTH), F32),
            pltpu.SemaphoreType.DMA((WIDTH // SPAN,)),
            pltpu.SemaphoreType.DMA((GROUPS,)),
        ],
        compiler_params=params(12),
    )(ids, ancestors, flat)
    coeff = pl.pallas_call(
        coeff_kernel,
        out_shape=shape((MSG, SPAN)),
        in_specs=[SMEM, VMEM, VMEM, VMEM, ANY],
        out_specs=VMEM,
        compiler_params=params(8),
    )(ids, adjacency.T, conductance, vertical, sent)
    c_far = lax.ppermute(coeff, "tile", x_pairs(0))
    c_near = [coeff] + [lax.ppermute(coeff, "tile", z_pairs(s)) for s in range(1, RING)]
    c_far = [c_far] + [lax.ppermute(c_far, "tile", z_pairs(s)) for s in range(1, RING)]
    c_mine = jnp.stack(c_near + c_far)
    got = lax.all_to_all(sent, "dom", split_axis=0, concat_axis=0, tiled=True)

    mine = pl.pallas_call(
        pack_kernel,
        out_shape=[shape((WIDTH // SPAN, ROWS + 8, SPAN))] * RING,
        in_specs=[SMEM, SMEM, VMEM, ANY],
        out_specs=[ANY] * RING,
        scratch_shapes=[
            pltpu.VMEM((2 * GROUPS, LAYERS, WIDTH), F32),
            pltpu.VMEM((RING, WIDTH // SPAN, ROWS + 8, SPAN), F32),
            pltpu.SMEM((GROUPS,), jnp.int32),
            pltpu.SemaphoreType.DMA,
            pltpu.SemaphoreType.DMA((RING,)),
        ],
        compiler_params=params(12),
    )(ids, ancestors, rainfall, got)
    ring = [mine[0]] + [lax.ppermute(mine[s], "tile", z_pairs(s)) for s in range(1, RING)]
    c_mine, *ring = lax.optimization_barrier((c_mine, *ring))
    c_other = lax.ppermute(c_mine, "dom", core_pairs())
    side = [lax.ppermute(ring[s], "tile", x_pairs(s)) for s in range(RING)]

    coefs = pl.pallas_call(
        expand_kernel,
        out_shape=[shape((PAIRS, 2, 4 * SPAN, 2 * SPAN), BF16), shape((PAIRS, 6 * HALF + 8, 2 * SPAN))],
        in_specs=[SMEM, VMEM, VMEM],
        out_specs=[VMEM] * 2,
        scratch_shapes=[pltpu.VMEM((PAIRS, LAYERS, 2 * SPAN), F32)],
        compiler_params=params(26),
    )(ids, c_mine, c_other)

    back = pl.pallas_call(
        step_kernel,
        out_shape=[shape((ROWS, WIDTH))] * RING,
        in_specs=[SMEM] + [VMEM] * 10,
        out_specs=[ANY] * RING,
        scratch_shapes=[pltpu.VMEM((2 * ROWS, (2 * PAIRS + 2) * SPAN), BF16)] * 2
        + [pltpu.VMEM((8, 2 * PAIRS * SPAN), F32)]
        + [pltpu.VMEM((ROWS, 2 * SPAN), F32)] * 4
        + [
            pltpu.VMEM((RING, ROWS, WIDTH), F32),
            pltpu.VMEM((PAIRS, 3 * HALF + 1, 8, 2 * SPAN), F32),
            pltpu.SemaphoreType.DMA((RING,)),
        ],
        compiler_params=params(46),
    )(ids, *ring, *side, *coefs)

    home = [back[0]] + [lax.ppermute(back[s], "tile", z_pairs(s)) for s in range(1, RING)]
    return pl.pallas_call(
        join_kernel,
        out_shape=shape((LAYERS, GROUP, WIDTH)),
        in_specs=[SMEM] + [ANY] * RING,
        out_specs=ANY,
        scratch_shapes=[
            pltpu.VMEM((RING, ROWS, WIDTH), F32),
            pltpu.VMEM((LAYERS, GROUP, WIDTH), F32),
            pltpu.SemaphoreType.DMA((RING,)),
            pltpu.SemaphoreType.DMA((8,)),
        ],
        compiler_params=params(14),
    )(ids, *home)


def solution(mesh):
    in_specs = (
        P(None, "dom", "tile"),
        P(),
        P(),
        P("tile", None, None, None),
        P(None, "tile"),
        P("dom", "tile"),
    )
    out_specs = P(None, "dom", "tile")
    return jax.shard_map(shards, mesh=mesh, in_specs=in_specs, out_specs=out_specs, check_vma=False)
```

```python
import jax
import jax.numpy as jnp
from jax import lax
from jax.experimental import pallas as pl
from jax.experimental.pallas import tpu as pltpu
from jax.sharding import PartitionSpec as P

SUBSTEPS = 8
RING = 4
OWN = 4
LAYERS = 64
HALF = 32
SPAN = 128
WIDTH = 512
GROUP = 16
GROUPS = 8
PAIRS = 16
ROWS = HALF * 8
MSG = 2 * (3 * SPAN + LAYERS)
F32 = jnp.float32
BF16 = jnp.bfloat16


def params(mib):
    return pltpu.CompilerParams(vmem_limit_bytes=mib * 1024 * 1024)


def shape(dims, dtype=F32):
    return jax.ShapeDtypeStruct(dims, dtype)


SMEM = pl.BlockSpec(memory_space=pltpu.SMEM)
VMEM = pl.BlockSpec(memory_space=pltpu.VMEM)
ANY = pl.BlockSpec(memory_space=pl.ANY)


def z_pairs(s):
    return [(4 * x + z, 4 * x + (z + s) % 4) for x in range(4) for z in range(4)]


def x_pairs(s):
    out = []
    for x in range(4):
        for z in range(4):
            step = -1 if (z - s) % 4 < 2 else 1
            out.append((4 * x + z, 4 * ((x + step) % 4) + z))
    return out


def row_pairs(step):
    return [(4 * x + z, 4 * ((x + step) % 4) + z) for x in range(4) for z in range(4)]


def core_pairs():
    return [(g, g ^ 1) for g in range(GROUPS)]


def send_kernel(ids, anc, moist, out, held, ready, sems, out_sems):
    copies = []
    for t in range(WIDTH // SPAN):
        copies.append(pltpu.make_async_copy(moist.at[:, pl.ds(t * SPAN, SPAN)], held.at[t], sems.at[t]))
        copies[-1].start()
    mine = ids[1]
    flip = 7 - lax.broadcasted_iota(jnp.int32, (8, SPAN), 0)
    picks = []
    for target in range(GROUPS):
        low = jnp.int32(GROUP)
        high = jnp.int32(-1)
        for i in range(GROUP):
            v = anc[target * GROUP + i] - mine * GROUP
            inside = (v >= 0) & (v < GROUP)
            low = jnp.where(inside, jnp.minimum(low, v), low)
            high = jnp.where(inside, jnp.maximum(high, v), high)
        picks.append((jnp.minimum(low, GROUP - 1), jnp.maximum(high, 0)))
    for c in copies:
        c.wait()
    leave = []
    for r in range(GROUPS):
        for j in range(2):
            for t in range(WIDTH // SPAN):
                lanes = slice(t * SPAN, (t + 1) * SPAN)
                rows = held[t, pl.ds(picks[r][j], LAYERS, stride=GROUP), :]
                ready[2 * r + j, :HALF, lanes] = rows[:HALF]
                for q in range(HALF // 8):
                    part = rows[LAYERS - 8 * (q + 1):LAYERS - 8 * q]
                    ready[2 * r + j, HALF + 8 * q:HALF + 8 * (q + 1), lanes] = jnp.take_along_axis(part, flip, axis=0)
        span = pl.ds(2 * r, 2)
        leave.append(pltpu.make_async_copy(ready.at[span], out.at[span], out_sems.at[r]))
        leave[-1].start()
    for c in leave:
        c.wait()


def pack_kernel(ids, anc, rain, *refs):
    arrived, outs = refs[0], refs[1:1 + RING]
    slots, ready, least, sem, out_sems = refs[1 + RING:]
    fetch = pltpu.make_async_copy(arrived, slots, sem)
    fetch.start()
    z = lax.rem(ids[0], RING)
    mine = ids[1]
    for g in range(GROUPS):
        least[g] = jnp.int32(1 << 20)
    for i in range(GROUP):
        v = anc[mine * GROUP + i]
        g = v // GROUP
        least[g] = jnp.minimum(least[g], v)
    fetch.wait()
    upper = lax.broadcasted_iota(jnp.int32, (8, WIDTH), 0) < 4
    leave = []
    for s in list(range(1, RING)) + [0]:
        owner = lax.rem(z + s, RING)
        for p in range(OWN):
            v = anc[mine * GROUP + owner * OWN + p]
            g = v // GROUP
            slot = 2 * g + jnp.where(v > least[g], 1, 0)
            for t in range(WIDTH // SPAN):
                lanes = slice(t * SPAN, (t + 1) * SPAN)
                for d in range(2):
                    ready[s, t, pl.ds(4 * d + p, HALF, stride=8), :] = slots[slot, d * HALF:(d + 1) * HALF, lanes]
        own_rain = rain[pl.ds(pl.multiple_of(owner // 2 * 8, 8), 8), :]
        own_rain = jnp.where(lax.rem(owner, 2) == 1, pltpu.roll(own_rain, 4, 0), own_rain)
        own_rain = jnp.where(upper, own_rain, 0.0)
        for t in range(WIDTH // SPAN):
            ready[s, t, ROWS:, :] = own_rain[:, t * SPAN:(t + 1) * SPAN]
        leave.append(pltpu.make_async_copy(ready.at[s], outs[s], out_sems.at[s]))
        leave[-1].start()
    for c in leave:
        c.wait()


def coeff_kernel(ids, adj, cond, vert, after, out):
    tile = ids[0]
    core = lax.rem(ids[1], 2)
    eye = (lax.broadcasted_iota(jnp.int32, (SPAN, SPAN), 0) == lax.broadcasted_iota(jnp.int32, (SPAN, SPAN), 1)).astype(F32)
    links = adj[...]
    block = lax.broadcasted_iota(jnp.int32, links.shape, 1)
    place = lax.broadcasted_iota(jnp.int32, links.shape, 0)
    other = jnp.where(links == block, 0.0, 1.0).astype(F32)
    for i in range(2):
        local = 2 * core + i
        b = RING * tile + local
        prev = jnp.sum(jnp.where((block == b) & (place == 1), other, 0.0))
        after = jnp.sum(jnp.where((block == b) & (place == 2), other, 0.0))
        own, first, second = cond[local, 0], cond[local, 1], cond[local, 2]
        base = i * (3 * SPAN + LAYERS)
        out[base:base + SPAN, :] = (first * prev).T
        out[base + SPAN:base + 2 * SPAN, :] = (own + first * (1.0 - prev) + second * (1.0 - after)).T + eye
        out[base + 2 * SPAN:base + 3 * SPAN, :] = (second * after).T
        lanes = pl.ds(pl.multiple_of(local * SPAN, SPAN), SPAN)
        out[base + 3 * SPAN:base + 3 * SPAN + LAYERS - 1, :] = vert[:, lanes]
        out[base + 3 * SPAN + LAYERS - 1:base + 3 * SPAN + LAYERS, :] = jnp.zeros((1, SPAN), F32)


def window_base(z, s, halo):
    t = lax.rem(z - s + RING, RING)
    if halo:
        return jnp.where(t < 2, 24 + 4 * t, 4 * t - 8)
    return 8 + 4 * t


def order_kernel(ids, *refs):
    ins, tiles, halves, sems, half_sems = refs[:RING], refs[RING], refs[RING + 1:RING + 3], refs[RING + 3], refs[RING + 4]
    z = lax.rem(ids[0], RING)
    copies = []
    for s in range(RING):
        t = lax.rem(z - s + RING, RING)
        copies.append(pltpu.make_async_copy(ins[s], tiles.at[t], sems.at[s]))
        copies[-1].start()
        for h in range(2):
            @pl.when(t // 2 == h)
            def _(s=s, t=t, h=h):
                pltpu.make_async_copy(ins[s], halves[h].at[t - 2 * h], half_sems.at[s]).start()
    for s in range(RING):
        copies[s].wait()
        pltpu.make_async_copy(ins[s], halves[0].at[0], half_sems.at[s]).wait()


def expand_kernel(ids, *refs):
    msgs = refs[:6]
    w_ref, c_ref, vs = refs[6:]
    core = lax.rem(ids[1], 2)
    for part, (start, tiles) in enumerate(((4, 4), (12, 2), (0, 2))):
        for at in range(tiles):
            for other in range(2):
                msg = msgs[2 * part + other]
                k = start + 2 * at + (core if other == 0 else 1 - core)
                for i in range(2):
                    row = i * (3 * SPAN + LAYERS)
                    cols = slice(i * SPAN, (i + 1) * SPAN)
                    rows = slice(i * SPAN, (i + 3) * SPAN)
                    w = msg[at, row:row + 3 * SPAN, :]
                    hi = w.astype(BF16)
                    w_ref[k, 0, rows, cols] = hi
                    w_ref[k, 1, rows, cols] = (w - hi.astype(F32)).astype(BF16)
                    empty = slice(3 * SPAN, 4 * SPAN) if i == 0 else slice(0, SPAN)
                    w_ref[k, 0, empty, cols] = jnp.zeros((SPAN, SPAN), BF16)
                    w_ref[k, 1, empty, cols] = jnp.zeros((SPAN, SPAN), BF16)
                    vs[k, :, i * SPAN:(i + 1) * SPAN] = msg[at, row + 3 * SPAN:row + 3 * SPAN + LAYERS, :]
    first = lax.broadcasted_iota(jnp.int32, (2, 2 * SPAN), 0) == 0
    group = 8

    def chunk(c, _):
        e_prev = [jnp.zeros((2, 2 * SPAN), F32)] * group
        for l in range(HALF):
            for q in range(group):
                k = c * group + q
                a_low = vs[k, LAYERS - 1 - l:LAYERS - l, :]
                a_top = vs[k, l - 1:l, :] if l else jnp.zeros((1, 2 * SPAN), F32)
                a = jnp.where(first, a_top, a_low)
                b = jnp.where(first, vs[k, l:l + 1, :], vs[k, LAYERS - 2 - l:LAYERS - 1 - l, :])
                inv = 1.0 / (1.0 + a + b - a * e_prev[q])
                e = b * inv
                c_ref[k, 2 * l:2 * l + 2] = inv
                c_ref[k, 2 * (HALF + l):2 * (HALF + l) + 2] = a * inv
                c_ref[k, 2 * (2 * HALF + l):2 * (2 * HALF + l) + 2] = e
                e_prev[q] = e
        for q in range(group):
            e = e_prev[q]
            both = 1.0 / (1.0 - e[0:1] * e[1:2])
            c_ref[c * group + q, 6 * HALF:6 * HALF + 8] = jnp.broadcast_to(both, (8, 2 * SPAN))
        return 0

    lax.fori_loop(0, PAIRS // group, chunk, 0)


def step_kernel(ids, *refs):
    ins, w, packed, outs = refs[:8], refs[8], refs[9], refs[10:14]
    x0, x1, rain, r_a, r_b, r_c, r_d, final, c, sems = refs[14:]
    z = lax.rem(ids[0], RING)
    upper = lax.broadcasted_iota(jnp.int32, (8, 2 * SPAN), 0) < 4

    def spread(k):
        for l in range(3 * HALF):
            c[k, l] = jnp.where(upper, packed[k, 2 * l:2 * l + 1, :], packed[k, 2 * l + 1:2 * l + 2, :])
        c[k, 3 * HALF] = packed[k, 6 * HALF:6 * HALF + 8, :]

    pad = jnp.zeros((2 * ROWS, SPAN), BF16)
    x0[:, :SPAN] = pad
    x0[:, (2 * PAIRS + 1) * SPAN:] = pad
    at = 0
    for halo in (False, True):
        for s in range(RING):
            base = window_base(z, s, halo)
            for t in range(WIDTH // SPAN):
                lanes = pl.ds(pl.multiple_of((base + 1 + t) * SPAN, SPAN), SPAN)
                v = ins[at][t, :ROWS, :]
                hi = v.astype(BF16)
                x0[:ROWS, lanes] = hi
                x0[ROWS:, lanes] = (v - hi.astype(F32)).astype(BF16)
                rain[:, pl.ds(pl.multiple_of((base + t) * SPAN, SPAN), SPAN)] = ins[at][t, ROWS:, :]
            at += 1

    def product(k, x, r):
        lanes = pl.ds(pl.multiple_of(k * 2 * SPAN, 2 * SPAN), 4 * SPAN)
        both = jnp.dot(x[:, lanes], w[k, 0], preferred_element_type=F32)
        acc = jnp.dot(x[:ROWS, lanes], w[k, 1], preferred_element_type=F32)
        acc = both[:ROWS] + (both[ROWS:] + acc)
        r[...] = acc
        r[:8, :] = acc[:8, :] + rain[:, pl.ds(pl.multiple_of(k * 2 * SPAN, 2 * SPAN), 2 * SPAN)]

    def forward(k, rs):
        ys = [r[:8, :] * c[k + q, 0] for q, r in enumerate(rs)]
        for q, r in enumerate(rs):
            r[:8, :] = ys[q]
        for l in range(1, HALF):
            for q, r in enumerate(rs):
                ys[q] = r[8 * l:8 * l + 8, :] * c[k + q, l] + c[k + q, HALF + l] * ys[q]
                if l < HALF - 1:
                    r[8 * l:8 * l + 8, :] = ys[q]
        return ys

    def backward(k, rs, ys, put):
        xs = [(y + c[k + q, 3 * HALF - 1] * pltpu.roll(y, 4, 0)) * c[k + q, 3 * HALF] for q, y in enumerate(ys)]
        later = list(xs)
        for l in range(HALF - 2, -1, -1):
            for q, r in enumerate(rs):
                xs[q] = r[8 * l:8 * l + 8, :] + c[k + q, 2 * HALF + l] * xs[q]
                if l % 2:
                    later[q] = xs[q]
                else:
                    put(k + q, l // 2, jnp.concatenate([xs[q], later[q]], axis=0))

    for step in range(1, SUBSTEPS + 1):
        src, dst = (x0, x1) if step % 2 else (x1, x0)
        first, last = step // 2, PAIRS - step // 2
        groups = (last - first) // 2

        def put(k, m, v, dst=dst):
            lanes = pl.ds(pl.multiple_of((2 * k + 1) * SPAN, SPAN), 2 * SPAN)
            hi = v.astype(BF16)
            dst[16 * m:16 * m + 16, lanes] = hi
            dst[ROWS + 16 * m:ROWS + 16 * m + 16, lanes] = (v - hi.astype(F32)).astype(BF16)

        def put_final(k, m, v):
            t = (k - 4) // 2
            s = lax.rem(t - z + RING, RING)
            lanes = pl.ds(pl.multiple_of(lax.rem(k, 2) * 2 * SPAN, 2 * SPAN), 2 * SPAN)
            final[s, 16 * m:16 * m + 16, lanes] = v

        write = put_final if step == SUBSTEPS else put

        def one(k, r, src=src):
            product(k, src, r)

        def ready(k, n, step=step):
            if step == 1:
                for q in range(n):
                    spread(k + q)

        near, far = (r_a, r_b), (r_c, r_d)
        one(first, r_a)
        one(first + 1, r_b)

        def body(i, _, first=first, one=one, ready=ready, write=write):
            k = first + 4 * i
            for at, (old, new) in ((k, (near, far)), (k + 2, (far, near))):
                ready(at, 2)
                one(at + 2, new[0])
                ys = forward(at, old)
                one(at + 3, new[1])
                backward(at, old, ys, write)
            return 0

        lax.fori_loop(0, (groups - 1) // 2, body, 0)
        rest = [(last - 2, near)]
        if groups % 2 == 0:
            ready(last - 4, 2)
            one(last - 2, r_c)
            ys = forward(last - 4, near)
            one(last - 1, r_d)
            backward(last - 4, near, ys, write)
            rest = [(last - 2, far)]
        for at, old in rest:
            ready(at, 2)
            backward(at, old, forward(at, old), write)

    copies = [pltpu.make_async_copy(final.at[s], outs[s], sems.at[s]) for s in range(RING)]
    for c_out in copies:
        c_out.start()
    for c_out in copies:
        c_out.wait()


def join_kernel(ids, *refs):
    ins, out, held, ready, sems, out_sems = refs[:RING], *refs[RING:]
    z = lax.rem(ids[0], RING)
    copies = []
    for s in range(RING):
        copies.append(pltpu.make_async_copy(ins[s], held.at[lax.rem(z - s + RING, RING)], sems.at[s]))
        copies[-1].start()
    for c in copies:
        c.wait()
    upper = lax.broadcasted_iota(jnp.int32, (8, WIDTH), 0) < 4
    parts = 4
    depth = HALF // parts
    leave = []
    for part in range(parts):
        for l in range(part * depth, (part + 1) * depth):
            for h in range(2):
                a = held[2 * h, 8 * l:8 * l + 8, :]
                b = held[2 * h + 1, 8 * l:8 * l + 8, :]
                ready[l, 8 * h:8 * h + 8, :] = jnp.where(upper, a, pltpu.roll(b, 4, 0))
                ready[LAYERS - 1 - l, 8 * h:8 * h + 8, :] = jnp.where(upper, pltpu.roll(a, 4, 0), b)
        for i, low in enumerate((part * depth, LAYERS - (part + 1) * depth)):
            span = pl.ds(low, depth)
            leave.append(pltpu.make_async_copy(ready.at[span], out.at[span], out_sems.at[2 * part + i]))
            leave[-1].start()
    for c in leave:
        c.wait()


def shards(moisture, ancestors, adjacency, conductance, vertical, rainfall):
    ids = jnp.stack([lax.axis_index("tile"), lax.axis_index("dom")]).astype(jnp.int32)

    flat = moisture.reshape(LAYERS * GROUP, WIDTH)
    sent = pl.pallas_call(
        send_kernel,
        out_shape=shape((2 * GROUPS, LAYERS, WIDTH)),
        in_specs=[SMEM, SMEM, ANY],
        out_specs=ANY,
        scratch_shapes=[
            pltpu.VMEM((WIDTH // SPAN, LAYERS * GROUP, SPAN), F32),
            pltpu.VMEM((2 * GROUPS, LAYERS, WIDTH), F32),
            pltpu.SemaphoreType.DMA((WIDTH // SPAN,)),
            pltpu.SemaphoreType.DMA((GROUPS,)),
        ],
        compiler_params=params(12),
    )(ids, ancestors, flat)
    coeff = pl.pallas_call(
        coeff_kernel,
        out_shape=shape((MSG, SPAN)),
        in_specs=[SMEM, VMEM, VMEM, VMEM, ANY],
        out_specs=VMEM,
        compiler_params=params(8),
    )(ids, adjacency.T, conductance, vertical, sent)
    c_ring = [coeff] + [lax.ppermute(coeff, "tile", z_pairs(s)) for s in range(1, RING)]
    c_tiles, c_low, c_high = pl.pallas_call(
        order_kernel,
        out_shape=[shape((RING, MSG, SPAN)), shape((2, MSG, SPAN)), shape((2, MSG, SPAN))],
        in_specs=[SMEM] + [ANY] * RING,
        out_specs=[ANY] * 3,
        scratch_shapes=[pltpu.SemaphoreType.DMA((RING,)), pltpu.SemaphoreType.DMA((RING,))],
        compiler_params=params(4),
    )(ids, *c_ring)
    c_parts = [c_tiles, lax.ppermute(c_low, "tile", row_pairs(-1)), lax.ppermute(c_high, "tile", row_pairs(1))]
    got = lax.all_to_all(sent, "dom", split_axis=0, concat_axis=0, tiled=True)

    mine = pl.pallas_call(
        pack_kernel,
        out_shape=[shape((WIDTH // SPAN, ROWS + 8, SPAN))] * RING,
        in_specs=[SMEM, SMEM, VMEM, ANY],
        out_specs=[ANY] * RING,
        scratch_shapes=[
            pltpu.VMEM((2 * GROUPS, LAYERS, WIDTH), F32),
            pltpu.VMEM((RING, WIDTH // SPAN, ROWS + 8, SPAN), F32),
            pltpu.SMEM((GROUPS,), jnp.int32),
            pltpu.SemaphoreType.DMA,
            pltpu.SemaphoreType.DMA((RING,)),
        ],
        compiler_params=params(12),
    )(ids, ancestors, rainfall, got)
    ring = [mine[0]] + [lax.ppermute(mine[s], "tile", z_pairs(s)) for s in range(1, RING)]
    *c_parts, ring[0], ring[1], ring[2], ring[3] = lax.optimization_barrier((*c_parts, *ring))
    c_all = []
    for c in c_parts:
        c_all += [c, lax.ppermute(c, "dom", core_pairs())]
    side = [lax.ppermute(ring[s], "tile", x_pairs(s)) for s in range(RING)]

    coefs = pl.pallas_call(
        expand_kernel,
        out_shape=[shape((PAIRS, 2, 4 * SPAN, 2 * SPAN), BF16), shape((PAIRS, 6 * HALF + 8, 2 * SPAN))],
        in_specs=[SMEM] + [VMEM] * 6,
        out_specs=[VMEM] * 2,
        scratch_shapes=[pltpu.VMEM((PAIRS, LAYERS, 2 * SPAN), F32)],
        compiler_params=params(26),
    )(ids, *c_all)

    back = pl.pallas_call(
        step_kernel,
        out_shape=[shape((ROWS, WIDTH))] * RING,
        in_specs=[SMEM] + [VMEM] * 10,
        out_specs=[ANY] * RING,
        scratch_shapes=[pltpu.VMEM((2 * ROWS, (2 * PAIRS + 2) * SPAN), BF16)] * 2
        + [pltpu.VMEM((8, 2 * PAIRS * SPAN), F32)]
        + [pltpu.VMEM((ROWS, 2 * SPAN), F32)] * 4
        + [
            pltpu.VMEM((RING, ROWS, WIDTH), F32),
            pltpu.VMEM((PAIRS, 3 * HALF + 1, 8, 2 * SPAN), F32),
            pltpu.SemaphoreType.DMA((RING,)),
        ],
        compiler_params=params(46),
    )(ids, *ring, *side, *coefs)

    home = [back[0]] + [lax.ppermute(back[s], "tile", z_pairs(s)) for s in range(1, RING)]
    return pl.pallas_call(
        join_kernel,
        out_shape=shape((LAYERS, GROUP, WIDTH)),
        in_specs=[SMEM] + [ANY] * RING,
        out_specs=ANY,
        scratch_shapes=[
            pltpu.VMEM((RING, ROWS, WIDTH), F32),
            pltpu.VMEM((LAYERS, GROUP, WIDTH), F32),
            pltpu.SemaphoreType.DMA((RING,)),
            pltpu.SemaphoreType.DMA((8,)),
        ],
        compiler_params=params(14),
    )(ids, *home)


def solution(mesh):
    in_specs = (
        P(None, "dom", "tile"),
        P(),
        P(),
        P("tile", None, None, None),
        P(None, "tile"),
        P("dom", "tile"),
    )
    out_specs = P(None, "dom", "tile")
    return jax.shard_map(shards, mesh=mesh, in_specs=in_specs, out_specs=out_specs, check_vma=False)
```

```python
import jax
import jax.numpy as jnp
from jax import lax
from jax.experimental import pallas as pl
from jax.experimental.pallas import tpu as pltpu
from jax.sharding import PartitionSpec as P

SUBSTEPS = 8
RING = 4
OWN = 4
LAYERS = 64
HALF = 32
SPAN = 128
WIDTH = 512
GROUP = 16
GROUPS = 8
PAIRS = 16
ROWS = HALF * 8
MSG = 2 * (3 * SPAN + LAYERS)
F32 = jnp.float32
BF16 = jnp.bfloat16


def params(mib):
    return pltpu.CompilerParams(vmem_limit_bytes=mib * 1024 * 1024)


def shape(dims, dtype=F32):
    return jax.ShapeDtypeStruct(dims, dtype)


SMEM = pl.BlockSpec(memory_space=pltpu.SMEM)
VMEM = pl.BlockSpec(memory_space=pltpu.VMEM)
ANY = pl.BlockSpec(memory_space=pl.ANY)


def z_pairs(s):
    return [(4 * x + z, 4 * x + (z + s) % 4) for x in range(4) for z in range(4)]


def x_pairs(s):
    out = []
    for x in range(4):
        for z in range(4):
            step = -1 if (z - s) % 4 < 2 else 1
            out.append((4 * x + z, 4 * ((x + step) % 4) + z))
    return out


def row_pairs(step):
    return [(4 * x + z, 4 * ((x + step) % 4) + z) for x in range(4) for z in range(4)]


def core_pairs():
    return [(g, g ^ 1) for g in range(GROUPS)]


def send_kernel(ids, anc, moist, out, held, ready, sems, out_sems):
    copies = []
    for t in range(WIDTH // SPAN):
        copies.append(pltpu.make_async_copy(moist.at[:, pl.ds(t * SPAN, SPAN)], held.at[t], sems.at[t]))
        copies[-1].start()
    mine = ids[1]
    flip = 7 - lax.broadcasted_iota(jnp.int32, (8, SPAN), 0)
    picks = []
    for target in range(GROUPS):
        low = jnp.int32(GROUP)
        high = jnp.int32(-1)
        for i in range(GROUP):
            v = anc[target * GROUP + i] - mine * GROUP
            inside = (v >= 0) & (v < GROUP)
            low = jnp.where(inside, jnp.minimum(low, v), low)
            high = jnp.where(inside, jnp.maximum(high, v), high)
        picks.append((jnp.minimum(low, GROUP - 1), jnp.maximum(high, 0)))
    for c in copies:
        c.wait()
    leave = []
    for r in range(GROUPS):
        for j in range(2):
            for t in range(WIDTH // SPAN):
                lanes = slice(t * SPAN, (t + 1) * SPAN)
                rows = held[t, pl.ds(picks[r][j], LAYERS, stride=GROUP), :]
                ready[2 * r + j, :HALF, lanes] = rows[:HALF]
                for q in range(HALF // 8):
                    part = rows[LAYERS - 8 * (q + 1):LAYERS - 8 * q]
                    ready[2 * r + j, HALF + 8 * q:HALF + 8 * (q + 1), lanes] = jnp.take_along_axis(part, flip, axis=0)
        span = pl.ds(2 * r, 2)
        leave.append(pltpu.make_async_copy(ready.at[span], out.at[span], out_sems.at[r]))
        leave[-1].start()
    for c in leave:
        c.wait()


def pack_kernel(ids, anc, rain, *refs):
    arrived, outs = refs[0], refs[1:1 + RING]
    slots, ready, least, sem, out_sems = refs[1 + RING:]
    fetch = pltpu.make_async_copy(arrived, slots, sem)
    fetch.start()
    z = lax.rem(ids[0], RING)
    mine = ids[1]
    for g in range(GROUPS):
        least[g] = jnp.int32(1 << 20)
    for i in range(GROUP):
        v = anc[mine * GROUP + i]
        g = v // GROUP
        least[g] = jnp.minimum(least[g], v)
    fetch.wait()
    upper = lax.broadcasted_iota(jnp.int32, (8, WIDTH), 0) < 4
    leave = []
    for s in list(range(1, RING)) + [0]:
        owner = lax.rem(z + s, RING)
        for p in range(OWN):
            v = anc[mine * GROUP + owner * OWN + p]
            g = v // GROUP
            slot = 2 * g + jnp.where(v > least[g], 1, 0)
            for t in range(WIDTH // SPAN):
                lanes = slice(t * SPAN, (t + 1) * SPAN)
                for d in range(2):
                    ready[s, t, pl.ds(4 * d + p, HALF, stride=8), :] = slots[slot, d * HALF:(d + 1) * HALF, lanes]
        own_rain = rain[pl.ds(pl.multiple_of(owner // 2 * 8, 8), 8), :]
        own_rain = jnp.where(lax.rem(owner, 2) == 1, pltpu.roll(own_rain, 4, 0), own_rain)
        own_rain = jnp.where(upper, own_rain, 0.0)
        for t in range(WIDTH // SPAN):
            ready[s, t, ROWS:, :] = own_rain[:, t * SPAN:(t + 1) * SPAN]
        leave.append(pltpu.make_async_copy(ready.at[s], outs[s], out_sems.at[s]))
        leave[-1].start()
    for c in leave:
        c.wait()


def coeff_kernel(ids, adj, cond, vert, after, out):
    tile = ids[0]
    core = lax.rem(ids[1], 2)
    eye = (lax.broadcasted_iota(jnp.int32, (SPAN, SPAN), 0) == lax.broadcasted_iota(jnp.int32, (SPAN, SPAN), 1)).astype(F32)
    links = adj[...]
    block = lax.broadcasted_iota(jnp.int32, links.shape, 1)
    place = lax.broadcasted_iota(jnp.int32, links.shape, 0)
    other = jnp.where(links == block, 0.0, 1.0).astype(F32)
    for i in range(2):
        local = 2 * core + i
        b = RING * tile + local
        prev = jnp.sum(jnp.where((block == b) & (place == 1), other, 0.0))
        after = jnp.sum(jnp.where((block == b) & (place == 2), other, 0.0))
        own, first, second = cond[local, 0], cond[local, 1], cond[local, 2]
        base = i * (3 * SPAN + LAYERS)
        out[base:base + SPAN, :] = (first * prev).T
        out[base + SPAN:base + 2 * SPAN, :] = (own + first * (1.0 - prev) + second * (1.0 - after)).T + eye
        out[base + 2 * SPAN:base + 3 * SPAN, :] = (second * after).T
        lanes = pl.ds(pl.multiple_of(local * SPAN, SPAN), SPAN)
        out[base + 3 * SPAN:base + 3 * SPAN + LAYERS - 1, :] = vert[:, lanes]
        out[base + 3 * SPAN + LAYERS - 1:base + 3 * SPAN + LAYERS, :] = jnp.zeros((1, SPAN), F32)


def window_base(z, s, halo):
    t = lax.rem(z - s + RING, RING)
    if halo:
        return jnp.where(t < 2, 24 + 4 * t, 4 * t - 8)
    return 8 + 4 * t


def order_kernel(ids, *refs):
    ins, tiles, halves, sems, half_sems = refs[:RING], refs[RING], refs[RING + 1:RING + 3], refs[RING + 3], refs[RING + 4]
    z = lax.rem(ids[0], RING)
    copies = []
    for s in range(RING):
        t = lax.rem(z - s + RING, RING)
        copies.append(pltpu.make_async_copy(ins[s], tiles.at[t], sems.at[s]))
        copies[-1].start()
        for h in range(2):
            @pl.when(t // 2 == h)
            def _(s=s, t=t, h=h):
                pltpu.make_async_copy(ins[s], halves[h].at[t - 2 * h], half_sems.at[s]).start()
    for s in range(RING):
        copies[s].wait()
        pltpu.make_async_copy(ins[s], halves[0].at[0], half_sems.at[s]).wait()


def edge_kernel(ids, *refs):
    ins, halves, sems = refs[:RING], refs[RING:RING + 2], refs[RING + 2]
    z = lax.rem(ids[0], RING)
    for s in range(RING):
        t = lax.rem(z - s + RING, RING)
        for h in range(2):
            @pl.when(t // 2 == h)
            def _(s=s, t=t, h=h):
                pltpu.make_async_copy(ins[s], halves[h].at[t - 2 * h], sems.at[s]).start()
    for s in range(RING):
        pltpu.make_async_copy(ins[s], halves[0].at[0], sems.at[s]).wait()


def expand_kernel(ids, *refs):
    msgs = refs[:6]
    w_ref, c_ref, vs = refs[6:]
    core = lax.rem(ids[1], 2)
    for part, (start, tiles) in enumerate(((4, 4), (12, 2), (0, 2))):
        for at in range(tiles):
            for other in range(2):
                msg = msgs[2 * part + other]
                k = start + 2 * at + (core if other == 0 else 1 - core)
                for i in range(2):
                    row = i * (3 * SPAN + LAYERS)
                    cols = slice(i * SPAN, (i + 1) * SPAN)
                    rows = slice(i * SPAN, (i + 3) * SPAN)
                    w = msg[at, row:row + 3 * SPAN, :]
                    hi = w.astype(BF16)
                    w_ref[k, 0, rows, cols] = hi
                    w_ref[k, 1, rows, cols] = (w - hi.astype(F32)).astype(BF16)
                    empty = slice(3 * SPAN, 4 * SPAN) if i == 0 else slice(0, SPAN)
                    w_ref[k, 0, empty, cols] = jnp.zeros((SPAN, SPAN), BF16)
                    w_ref[k, 1, empty, cols] = jnp.zeros((SPAN, SPAN), BF16)
                    vs[k, :, i * SPAN:(i + 1) * SPAN] = msg[at, row + 3 * SPAN:row + 3 * SPAN + LAYERS, :]
    first = lax.broadcasted_iota(jnp.int32, (2, 2 * SPAN), 0) == 0
    group = 8

    def chunk(c, _):
        e_prev = [jnp.zeros((2, 2 * SPAN), F32)] * group
        for l in range(HALF):
            for q in range(group):
                k = c * group + q
                a_low = vs[k, LAYERS - 1 - l:LAYERS - l, :]
                a_top = vs[k, l - 1:l, :] if l else jnp.zeros((1, 2 * SPAN), F32)
                a = jnp.where(first, a_top, a_low)
                b = jnp.where(first, vs[k, l:l + 1, :], vs[k, LAYERS - 2 - l:LAYERS - 1 - l, :])
                inv = 1.0 / (1.0 + a + b - a * e_prev[q])
                e = b * inv
                c_ref[k, 2 * l:2 * l + 2] = inv
                c_ref[k, 2 * (HALF + l):2 * (HALF + l) + 2] = a * inv
                c_ref[k, 2 * (2 * HALF + l):2 * (2 * HALF + l) + 2] = e
                e_prev[q] = e
        for q in range(group):
            e = e_prev[q]
            both = 1.0 / (1.0 - e[0:1] * e[1:2])
            c_ref[c * group + q, 6 * HALF:6 * HALF + 8] = jnp.broadcast_to(both, (8, 2 * SPAN))
        return 0

    lax.fori_loop(0, PAIRS // group, chunk, 0)


def step_kernel(ids, *refs):
    ins, side, w, packed, outs = refs[:4], refs[4:6], refs[6], refs[7], refs[8:12]
    x0, x1, rain, r_a, r_b, r_c, r_d, final, c, sems = refs[12:]
    z = lax.rem(ids[0], RING)
    upper = lax.broadcasted_iota(jnp.int32, (8, 2 * SPAN), 0) < 4

    def spread(k):
        for l in range(3 * HALF):
            c[k, l] = jnp.where(upper, packed[k, 2 * l:2 * l + 1, :], packed[k, 2 * l + 1:2 * l + 2, :])
        c[k, 3 * HALF] = packed[k, 6 * HALF:6 * HALF + 8, :]

    pad = jnp.zeros((2 * ROWS, SPAN), BF16)
    x0[:, :SPAN] = pad
    x0[:, (2 * PAIRS + 1) * SPAN:] = pad
    tiles = [(ins[s], window_base(z, s, False)) for s in range(RING)]
    tiles += [(side[0].at[t], 24 + 4 * t) for t in range(2)] + [(side[1].at[t], 4 * t) for t in range(2)]
    for src, base in tiles:
        for t in range(WIDTH // SPAN):
            lanes = pl.ds(pl.multiple_of((base + 1 + t) * SPAN, SPAN), SPAN)
            v = src[t, :ROWS, :]
            hi = v.astype(BF16)
            x0[:ROWS, lanes] = hi
            x0[ROWS:, lanes] = (v - hi.astype(F32)).astype(BF16)
            rain[:, pl.ds(pl.multiple_of((base + t) * SPAN, SPAN), SPAN)] = src[t, ROWS:, :]

    def product(k, x, r):
        lanes = pl.ds(pl.multiple_of(k * 2 * SPAN, 2 * SPAN), 4 * SPAN)
        both = jnp.dot(x[:, lanes], w[k, 0], preferred_element_type=F32)
        acc = jnp.dot(x[:ROWS, lanes], w[k, 1], preferred_element_type=F32)
        acc = both[:ROWS] + (both[ROWS:] + acc)
        r[...] = acc
        r[:8, :] = acc[:8, :] + rain[:, pl.ds(pl.multiple_of(k * 2 * SPAN, 2 * SPAN), 2 * SPAN)]

    def forward(k, rs):
        ys = [r[:8, :] * c[k + q, 0] for q, r in enumerate(rs)]
        for q, r in enumerate(rs):
            r[:8, :] = ys[q]
        for l in range(1, HALF):
            for q, r in enumerate(rs):
                ys[q] = r[8 * l:8 * l + 8, :] * c[k + q, l] + c[k + q, HALF + l] * ys[q]
                if l < HALF - 1:
                    r[8 * l:8 * l + 8, :] = ys[q]
        return ys

    def backward(k, rs, ys, put):
        xs = [(y + c[k + q, 3 * HALF - 1] * pltpu.roll(y, 4, 0)) * c[k + q, 3 * HALF] for q, y in enumerate(ys)]
        later = list(xs)
        for l in range(HALF - 2, -1, -1):
            for q, r in enumerate(rs):
                xs[q] = r[8 * l:8 * l + 8, :] + c[k + q, 2 * HALF + l] * xs[q]
                if l % 2:
                    later[q] = xs[q]
                else:
                    put(k + q, l // 2, jnp.concatenate([xs[q], later[q]], axis=0))

    for step in range(1, SUBSTEPS + 1):
        src, dst = (x0, x1) if step % 2 else (x1, x0)
        first, last = step // 2, PAIRS - step // 2
        groups = (last - first) // 2

        def put(k, m, v, dst=dst):
            lanes = pl.ds(pl.multiple_of((2 * k + 1) * SPAN, SPAN), 2 * SPAN)
            hi = v.astype(BF16)
            dst[16 * m:16 * m + 16, lanes] = hi
            dst[ROWS + 16 * m:ROWS + 16 * m + 16, lanes] = (v - hi.astype(F32)).astype(BF16)

        def put_final(k, m, v):
            t = (k - 4) // 2
            s = lax.rem(t - z + RING, RING)
            lanes = pl.ds(pl.multiple_of(lax.rem(k, 2) * 2 * SPAN, 2 * SPAN), 2 * SPAN)
            final[s, 16 * m:16 * m + 16, lanes] = v

        write = put_final if step == SUBSTEPS else put

        def one(k, r, src=src):
            product(k, src, r)

        def ready(k, n, step=step):
            if step == 1:
                for q in range(n):
                    spread(k + q)

        near, far = (r_a, r_b), (r_c, r_d)
        one(first, r_a)
        one(first + 1, r_b)

        def body(i, _, first=first, one=one, ready=ready, write=write):
            k = first + 4 * i
            for at, (old, new) in ((k, (near, far)), (k + 2, (far, near))):
                ready(at, 2)
                one(at + 2, new[0])
                ys = forward(at, old)
                one(at + 3, new[1])
                backward(at, old, ys, write)
            return 0

        lax.fori_loop(0, (groups - 1) // 2, body, 0)
        rest = [(last - 2, near)]
        if groups % 2 == 0:
            ready(last - 4, 2)
            one(last - 2, r_c)
            ys = forward(last - 4, near)
            one(last - 1, r_d)
            backward(last - 4, near, ys, write)
            rest = [(last - 2, far)]
        for at, old in rest:
            ready(at, 2)
            backward(at, old, forward(at, old), write)

    copies = [pltpu.make_async_copy(final.at[s], outs[s], sems.at[s]) for s in range(RING)]
    for c_out in copies:
        c_out.start()
    for c_out in copies:
        c_out.wait()


def join_kernel(ids, *refs):
    ins, out, held, ready, sems, out_sems = refs[:RING], *refs[RING:]
    z = lax.rem(ids[0], RING)
    copies = []
    for s in range(RING):
        copies.append(pltpu.make_async_copy(ins[s], held.at[lax.rem(z - s + RING, RING)], sems.at[s]))
        copies[-1].start()
    for c in copies:
        c.wait()
    upper = lax.broadcasted_iota(jnp.int32, (8, WIDTH), 0) < 4
    parts = 4
    depth = HALF // parts
    leave = []
    for part in range(parts):
        for l in range(part * depth, (part + 1) * depth):
            for h in range(2):
                a = held[2 * h, 8 * l:8 * l + 8, :]
                b = held[2 * h + 1, 8 * l:8 * l + 8, :]
                ready[l, 8 * h:8 * h + 8, :] = jnp.where(upper, a, pltpu.roll(b, 4, 0))
                ready[LAYERS - 1 - l, 8 * h:8 * h + 8, :] = jnp.where(upper, pltpu.roll(a, 4, 0), b)
        for i, low in enumerate((part * depth, LAYERS - (part + 1) * depth)):
            span = pl.ds(low, depth)
            leave.append(pltpu.make_async_copy(ready.at[span], out.at[span], out_sems.at[2 * part + i]))
            leave[-1].start()
    for c in leave:
        c.wait()


def shards(moisture, ancestors, adjacency, conductance, vertical, rainfall):
    ids = jnp.stack([lax.axis_index("tile"), lax.axis_index("dom")]).astype(jnp.int32)

    flat = moisture.reshape(LAYERS * GROUP, WIDTH)
    sent = pl.pallas_call(
        send_kernel,
        out_shape=shape((2 * GROUPS, LAYERS, WIDTH)),
        in_specs=[SMEM, SMEM, ANY],
        out_specs=ANY,
        scratch_shapes=[
            pltpu.VMEM((WIDTH // SPAN, LAYERS * GROUP, SPAN), F32),
            pltpu.VMEM((2 * GROUPS, LAYERS, WIDTH), F32),
            pltpu.SemaphoreType.DMA((WIDTH // SPAN,)),
            pltpu.SemaphoreType.DMA((GROUPS,)),
        ],
        compiler_params=params(12),
    )(ids, ancestors, flat)
    coeff = pl.pallas_call(
        coeff_kernel,
        out_shape=shape((MSG, SPAN)),
        in_specs=[SMEM, VMEM, VMEM, VMEM, ANY],
        out_specs=VMEM,
        compiler_params=params(8),
    )(ids, adjacency.T, conductance, vertical, sent)
    c_ring = [coeff] + [lax.ppermute(coeff, "tile", z_pairs(s)) for s in range(1, RING)]
    c_tiles, c_low, c_high = pl.pallas_call(
        order_kernel,
        out_shape=[shape((RING, MSG, SPAN)), shape((2, MSG, SPAN)), shape((2, MSG, SPAN))],
        in_specs=[SMEM] + [ANY] * RING,
        out_specs=[ANY] * 3,
        scratch_shapes=[pltpu.SemaphoreType.DMA((RING,)), pltpu.SemaphoreType.DMA((RING,))],
        compiler_params=params(4),
    )(ids, *c_ring)
    c_parts = [c_tiles, lax.ppermute(c_low, "tile", row_pairs(-1)), lax.ppermute(c_high, "tile", row_pairs(1))]
    got = lax.all_to_all(sent, "dom", split_axis=0, concat_axis=0, tiled=True)

    mine = pl.pallas_call(
        pack_kernel,
        out_shape=[shape((WIDTH // SPAN, ROWS + 8, SPAN))] * RING,
        in_specs=[SMEM, SMEM, VMEM, ANY],
        out_specs=[ANY] * RING,
        scratch_shapes=[
            pltpu.VMEM((2 * GROUPS, LAYERS, WIDTH), F32),
            pltpu.VMEM((RING, WIDTH // SPAN, ROWS + 8, SPAN), F32),
            pltpu.SMEM((GROUPS,), jnp.int32),
            pltpu.SemaphoreType.DMA,
            pltpu.SemaphoreType.DMA((RING,)),
        ],
        compiler_params=params(12),
    )(ids, ancestors, rainfall, got)
    ring = [mine[0]] + [lax.ppermute(mine[s], "tile", z_pairs(s)) for s in range(1, RING)]
    *c_parts, ring[0], ring[1], ring[2], ring[3] = lax.optimization_barrier((*c_parts, *ring))
    c_all = []
    for c in c_parts:
        c_all += [c, lax.ppermute(c, "dom", core_pairs())]
    state = (WIDTH // SPAN, ROWS + 8, SPAN)
    low, high = pl.pallas_call(
        edge_kernel,
        out_shape=[shape((2, *state)), shape((2, *state))],
        in_specs=[SMEM] + [ANY] * RING,
        out_specs=[ANY] * 2,
        scratch_shapes=[pltpu.SemaphoreType.DMA((RING,))],
        compiler_params=params(4),
    )(ids, *ring)
    side = [lax.ppermute(low, "tile", row_pairs(-1)), lax.ppermute(high, "tile", row_pairs(1))]

    coefs = pl.pallas_call(
        expand_kernel,
        out_shape=[shape((PAIRS, 2, 4 * SPAN, 2 * SPAN), BF16), shape((PAIRS, 6 * HALF + 8, 2 * SPAN))],
        in_specs=[SMEM] + [VMEM] * 6,
        out_specs=[VMEM] * 2,
        scratch_shapes=[pltpu.VMEM((PAIRS, LAYERS, 2 * SPAN), F32)],
        compiler_params=params(26),
    )(ids, *c_all)

    back = pl.pallas_call(
        step_kernel,
        out_shape=[shape((ROWS, WIDTH))] * RING,
        in_specs=[SMEM] + [VMEM] * 8,
        out_specs=[ANY] * RING,
        scratch_shapes=[pltpu.VMEM((2 * ROWS, (2 * PAIRS + 2) * SPAN), BF16)] * 2
        + [pltpu.VMEM((8, 2 * PAIRS * SPAN), F32)]
        + [pltpu.VMEM((ROWS, 2 * SPAN), F32)] * 4
        + [
            pltpu.VMEM((RING, ROWS, WIDTH), F32),
            pltpu.VMEM((PAIRS, 3 * HALF + 1, 8, 2 * SPAN), F32),
            pltpu.SemaphoreType.DMA((RING,)),
        ],
        compiler_params=params(46),
    )(ids, *ring, *side, *coefs)

    home = [back[0]] + [lax.ppermute(back[s], "tile", z_pairs(s)) for s in range(1, RING)]
    return pl.pallas_call(
        join_kernel,
        out_shape=shape((LAYERS, GROUP, WIDTH)),
        in_specs=[SMEM] + [ANY] * RING,
        out_specs=ANY,
        scratch_shapes=[
            pltpu.VMEM((RING, ROWS, WIDTH), F32),
            pltpu.VMEM((LAYERS, GROUP, WIDTH), F32),
            pltpu.SemaphoreType.DMA((RING,)),
            pltpu.SemaphoreType.DMA((8,)),
        ],
        compiler_params=params(14),
    )(ids, *home)


def solution(mesh):
    in_specs = (
        P(None, "dom", "tile"),
        P(),
        P(),
        P("tile", None, None, None),
        P(None, "tile"),
        P("dom", "tile"),
    )
    out_specs = P(None, "dom", "tile")
    return jax.shard_map(shards, mesh=mesh, in_specs=in_specs, out_specs=out_specs, check_vma=False)
```

```python
import jax
import jax.numpy as jnp
from jax import lax
from jax.experimental import pallas as pl
from jax.experimental.pallas import tpu as pltpu
from jax.sharding import PartitionSpec as P

SUBSTEPS = 8
RING = 4
OWN = 4
LAYERS = 64
HALF = 32
SPAN = 128
WIDTH = 512
GROUP = 16
GROUPS = 8
PAIRS = 16
ROWS = HALF * 8
MSG = 2 * (3 * SPAN + LAYERS)
F32 = jnp.float32
BF16 = jnp.bfloat16


def params(mib):
    return pltpu.CompilerParams(vmem_limit_bytes=mib * 1024 * 1024)


def shape(dims, dtype=F32):
    return jax.ShapeDtypeStruct(dims, dtype)


SMEM = pl.BlockSpec(memory_space=pltpu.SMEM)
VMEM = pl.BlockSpec(memory_space=pltpu.VMEM)
ANY = pl.BlockSpec(memory_space=pl.ANY)


def z_pairs(s):
    return [(4 * x + z, 4 * x + (z + s) % 4) for x in range(4) for z in range(4)]


def x_pairs(s):
    out = []
    for x in range(4):
        for z in range(4):
            step = -1 if (z - s) % 4 < 2 else 1
            out.append((4 * x + z, 4 * ((x + step) % 4) + z))
    return out


def row_pairs(step):
    return [(4 * x + z, 4 * ((x + step) % 4) + z) for x in range(4) for z in range(4)]


def core_pairs():
    return [(g, g ^ 1) for g in range(GROUPS)]


def send_kernel(ids, anc, moist, out, held, ready, sems, out_sems):
    copies = []
    for t in range(WIDTH // SPAN):
        copies.append(pltpu.make_async_copy(moist.at[:, pl.ds(t * SPAN, SPAN)], held.at[t], sems.at[t]))
        copies[-1].start()
    mine = ids[1]
    flip = 7 - lax.broadcasted_iota(jnp.int32, (8, SPAN), 0)
    picks = []
    for target in range(GROUPS):
        low = jnp.int32(GROUP)
        high = jnp.int32(-1)
        for i in range(GROUP):
            v = anc[target * GROUP + i] - mine * GROUP
            inside = (v >= 0) & (v < GROUP)
            low = jnp.where(inside, jnp.minimum(low, v), low)
            high = jnp.where(inside, jnp.maximum(high, v), high)
        picks.append((jnp.minimum(low, GROUP - 1), jnp.maximum(high, 0)))
    for c in copies:
        c.wait()
    leave = []
    for r in range(GROUPS):
        for j in range(2):
            for t in range(WIDTH // SPAN):
                lanes = slice(t * SPAN, (t + 1) * SPAN)
                rows = held[t, pl.ds(picks[r][j], LAYERS, stride=GROUP), :]
                ready[2 * r + j, :HALF, lanes] = rows[:HALF]
                for q in range(HALF // 8):
                    part = rows[LAYERS - 8 * (q + 1):LAYERS - 8 * q]
                    ready[2 * r + j, HALF + 8 * q:HALF + 8 * (q + 1), lanes] = jnp.take_along_axis(part, flip, axis=0)
        span = pl.ds(2 * r, 2)
        leave.append(pltpu.make_async_copy(ready.at[span], out.at[span], out_sems.at[r]))
        leave[-1].start()
    for c in leave:
        c.wait()


def pack_kernel(ids, anc, rain, *refs):
    arrived, outs = refs[0], refs[1:1 + RING]
    slots, ready, least, sem, out_sems = refs[1 + RING:]
    fetch = pltpu.make_async_copy(arrived, slots, sem)
    fetch.start()
    z = lax.rem(ids[0], RING)
    mine = ids[1]
    for g in range(GROUPS):
        least[g] = jnp.int32(1 << 20)
    for i in range(GROUP):
        v = anc[mine * GROUP + i]
        g = v // GROUP
        least[g] = jnp.minimum(least[g], v)
    fetch.wait()
    upper = lax.broadcasted_iota(jnp.int32, (8, WIDTH), 0) < 4
    leave = []
    for s in list(range(1, RING)) + [0]:
        owner = lax.rem(z + s, RING)
        for p in range(OWN):
            v = anc[mine * GROUP + owner * OWN + p]
            g = v // GROUP
            slot = 2 * g + jnp.where(v > least[g], 1, 0)
            for t in range(WIDTH // SPAN):
                lanes = slice(t * SPAN, (t + 1) * SPAN)
                for d in range(2):
                    ready[s, t, pl.ds(4 * d + p, HALF, stride=8), :] = slots[slot, d * HALF:(d + 1) * HALF, lanes]
        own_rain = rain[pl.ds(pl.multiple_of(owner // 2 * 8, 8), 8), :]
        own_rain = jnp.where(lax.rem(owner, 2) == 1, pltpu.roll(own_rain, 4, 0), own_rain)
        own_rain = jnp.where(upper, own_rain, 0.0)
        for t in range(WIDTH // SPAN):
            ready[s, t, ROWS:, :] = own_rain[:, t * SPAN:(t + 1) * SPAN]
        leave.append(pltpu.make_async_copy(ready.at[s], outs[s], out_sems.at[s]))
        leave[-1].start()
    for c in leave:
        c.wait()


def coeff_kernel(ids, adj, cond, vert, after, out):
    tile = ids[0]
    core = lax.rem(ids[1], 2)
    eye = (lax.broadcasted_iota(jnp.int32, (SPAN, SPAN), 0) == lax.broadcasted_iota(jnp.int32, (SPAN, SPAN), 1)).astype(F32)
    links = adj[...]
    block = lax.broadcasted_iota(jnp.int32, links.shape, 1)
    place = lax.broadcasted_iota(jnp.int32, links.shape, 0)
    other = jnp.where(links == block, 0.0, 1.0).astype(F32)
    for i in range(2):
        local = 2 * core + i
        b = RING * tile + local
        prev = jnp.sum(jnp.where((block == b) & (place == 1), other, 0.0))
        after = jnp.sum(jnp.where((block == b) & (place == 2), other, 0.0))
        own, first, second = cond[local, 0], cond[local, 1], cond[local, 2]
        base = i * (3 * SPAN + LAYERS)
        out[base:base + SPAN, :] = (first * prev).T
        out[base + SPAN:base + 2 * SPAN, :] = (own + first * (1.0 - prev) + second * (1.0 - after)).T + eye
        out[base + 2 * SPAN:base + 3 * SPAN, :] = (second * after).T
        lanes = pl.ds(pl.multiple_of(local * SPAN, SPAN), SPAN)
        out[base + 3 * SPAN:base + 3 * SPAN + LAYERS - 1, :] = vert[:, lanes]
        out[base + 3 * SPAN + LAYERS - 1:base + 3 * SPAN + LAYERS, :] = jnp.zeros((1, SPAN), F32)


def window_base(z, s, halo):
    t = lax.rem(z - s + RING, RING)
    if halo:
        return jnp.where(t < 2, 24 + 4 * t, 4 * t - 8)
    return 8 + 4 * t


def edge_kernel(ids, *refs):
    ins, halves, sems = refs[:RING], refs[RING:RING + 2], refs[RING + 2]
    z = lax.rem(ids[0], RING)
    for s in range(RING):
        t = lax.rem(z - s + RING, RING)
        for h in range(2):
            @pl.when(t // 2 == h)
            def _(s=s, t=t, h=h):
                pltpu.make_async_copy(ins[s], halves[h].at[t - 2 * h], sems.at[s]).start()
    for s in range(RING):
        pltpu.make_async_copy(ins[s], halves[0].at[0], sems.at[s]).wait()


def expand_kernel(ids, *refs):
    msgs = refs[:8]
    w_ref, c_ref, vs = refs[8:]
    core = lax.rem(ids[1], 2)
    for part, start in enumerate((4, 8, 12, 0)):
        for at in range(2):
            for other in range(2):
                msg = msgs[2 * part + other]
                k = start + 2 * at + (core if other == 0 else 1 - core)
                for i in range(2):
                    row = i * (3 * SPAN + LAYERS)
                    cols = slice(i * SPAN, (i + 1) * SPAN)
                    rows = slice(i * SPAN, (i + 3) * SPAN)
                    w = msg[at, row:row + 3 * SPAN, :]
                    hi = w.astype(BF16)
                    w_ref[k, 0, rows, cols] = hi
                    w_ref[k, 1, rows, cols] = (w - hi.astype(F32)).astype(BF16)
                    empty = slice(3 * SPAN, 4 * SPAN) if i == 0 else slice(0, SPAN)
                    w_ref[k, 0, empty, cols] = jnp.zeros((SPAN, SPAN), BF16)
                    w_ref[k, 1, empty, cols] = jnp.zeros((SPAN, SPAN), BF16)
                    vs[k, :, i * SPAN:(i + 1) * SPAN] = msg[at, row + 3 * SPAN:row + 3 * SPAN + LAYERS, :]
    first = lax.broadcasted_iota(jnp.int32, (2, 2 * SPAN), 0) == 0
    group = 8

    def chunk(c, _):
        e_prev = [jnp.zeros((2, 2 * SPAN), F32)] * group
        for l in range(HALF):
            for q in range(group):
                k = c * group + q
                a_low = vs[k, LAYERS - 1 - l:LAYERS - l, :]
                a_top = vs[k, l - 1:l, :] if l else jnp.zeros((1, 2 * SPAN), F32)
                a = jnp.where(first, a_top, a_low)
                b = jnp.where(first, vs[k, l:l + 1, :], vs[k, LAYERS - 2 - l:LAYERS - 1 - l, :])
                inv = 1.0 / (1.0 + a + b - a * e_prev[q])
                e = b * inv
                c_ref[k, 2 * l:2 * l + 2] = inv
                c_ref[k, 2 * (HALF + l):2 * (HALF + l) + 2] = a * inv
                c_ref[k, 2 * (2 * HALF + l):2 * (2 * HALF + l) + 2] = e
                e_prev[q] = e
        for q in range(group):
            e = e_prev[q]
            both = 1.0 / (1.0 - e[0:1] * e[1:2])
            c_ref[c * group + q, 6 * HALF:6 * HALF + 8] = jnp.broadcast_to(both, (8, 2 * SPAN))
        return 0

    lax.fori_loop(0, PAIRS // group, chunk, 0)


def step_kernel(ids, *refs):
    ins, side, w, packed, outs = refs[:4], refs[4:6], refs[6], refs[7], refs[8:12]
    x0, x1, rain, r_a, r_b, r_c, r_d, final, c, sems = refs[12:]
    z = lax.rem(ids[0], RING)
    upper = lax.broadcasted_iota(jnp.int32, (8, 2 * SPAN), 0) < 4

    def spread(k):
        for l in range(3 * HALF):
            c[k, l] = jnp.where(upper, packed[k, 2 * l:2 * l + 1, :], packed[k, 2 * l + 1:2 * l + 2, :])
        c[k, 3 * HALF] = packed[k, 6 * HALF:6 * HALF + 8, :]

    pad = jnp.zeros((2 * ROWS, SPAN), BF16)
    x0[:, :SPAN] = pad
    x0[:, (2 * PAIRS + 1) * SPAN:] = pad
    tiles = [(ins[s], window_base(z, s, False)) for s in range(RING)]
    tiles += [(side[0].at[t], 24 + 4 * t) for t in range(2)] + [(side[1].at[t], 4 * t) for t in range(2)]
    for src, base in tiles:
        for t in range(WIDTH // SPAN):
            lanes = pl.ds(pl.multiple_of((base + 1 + t) * SPAN, SPAN), SPAN)
            v = src[t, :ROWS, :]
            hi = v.astype(BF16)
            x0[:ROWS, lanes] = hi
            x0[ROWS:, lanes] = (v - hi.astype(F32)).astype(BF16)
            rain[:, pl.ds(pl.multiple_of((base + t) * SPAN, SPAN), SPAN)] = src[t, ROWS:, :]

    def product(k, x, r):
        lanes = pl.ds(pl.multiple_of(k * 2 * SPAN, 2 * SPAN), 4 * SPAN)
        both = jnp.dot(x[:, lanes], w[k, 0], preferred_element_type=F32)
        acc = jnp.dot(x[:ROWS, lanes], w[k, 1], preferred_element_type=F32)
        acc = both[:ROWS] + (both[ROWS:] + acc)
        r[...] = acc
        r[:8, :] = acc[:8, :] + rain[:, pl.ds(pl.multiple_of(k * 2 * SPAN, 2 * SPAN), 2 * SPAN)]

    def forward(k, rs):
        ys = [r[:8, :] * c[k + q, 0] for q, r in enumerate(rs)]
        for q, r in enumerate(rs):
            r[:8, :] = ys[q]
        for l in range(1, HALF):
            for q, r in enumerate(rs):
                ys[q] = r[8 * l:8 * l + 8, :] * c[k + q, l] + c[k + q, HALF + l] * ys[q]
                if l < HALF - 1:
                    r[8 * l:8 * l + 8, :] = ys[q]
        return ys

    def backward(k, rs, ys, put):
        xs = [(y + c[k + q, 3 * HALF - 1] * pltpu.roll(y, 4, 0)) * c[k + q, 3 * HALF] for q, y in enumerate(ys)]
        later = list(xs)
        for l in range(HALF - 2, -1, -1):
            for q, r in enumerate(rs):
                xs[q] = r[8 * l:8 * l + 8, :] + c[k + q, 2 * HALF + l] * xs[q]
                if l % 2:
                    later[q] = xs[q]
                else:
                    put(k + q, l // 2, jnp.concatenate([xs[q], later[q]], axis=0))

    for step in range(1, SUBSTEPS + 1):
        src, dst = (x0, x1) if step % 2 else (x1, x0)
        first, last = step // 2, PAIRS - step // 2
        groups = (last - first) // 2

        def put(k, m, v, dst=dst):
            lanes = pl.ds(pl.multiple_of((2 * k + 1) * SPAN, SPAN), 2 * SPAN)
            hi = v.astype(BF16)
            dst[16 * m:16 * m + 16, lanes] = hi
            dst[ROWS + 16 * m:ROWS + 16 * m + 16, lanes] = (v - hi.astype(F32)).astype(BF16)

        def put_final(k, m, v):
            t = (k - 4) // 2
            s = lax.rem(t - z + RING, RING)
            lanes = pl.ds(pl.multiple_of(lax.rem(k, 2) * 2 * SPAN, 2 * SPAN), 2 * SPAN)
            final[s, 16 * m:16 * m + 16, lanes] = v

        write = put_final if step == SUBSTEPS else put

        def one(k, r, src=src):
            product(k, src, r)

        def ready(k, n, step=step):
            if step == 1:
                for q in range(n):
                    spread(k + q)

        near, far = (r_a, r_b), (r_c, r_d)
        one(first, r_a)
        one(first + 1, r_b)

        def body(i, _, first=first, one=one, ready=ready, write=write):
            k = first + 4 * i
            for at, (old, new) in ((k, (near, far)), (k + 2, (far, near))):
                ready(at, 2)
                one(at + 2, new[0])
                ys = forward(at, old)
                one(at + 3, new[1])
                backward(at, old, ys, write)
            return 0

        lax.fori_loop(0, (groups - 1) // 2, body, 0)
        rest = [(last - 2, near)]
        if groups % 2 == 0:
            ready(last - 4, 2)
            one(last - 2, r_c)
            ys = forward(last - 4, near)
            one(last - 1, r_d)
            backward(last - 4, near, ys, write)
            rest = [(last - 2, far)]
        for at, old in rest:
            ready(at, 2)
            backward(at, old, forward(at, old), write)

    copies = [pltpu.make_async_copy(final.at[s], outs[s], sems.at[s]) for s in range(RING)]
    for c_out in copies:
        c_out.start()
    for c_out in copies:
        c_out.wait()


def join_kernel(ids, *refs):
    ins, out, held, ready, sems, out_sems = refs[:RING], *refs[RING:]
    z = lax.rem(ids[0], RING)
    copies = []
    for s in range(RING):
        copies.append(pltpu.make_async_copy(ins[s], held.at[lax.rem(z - s + RING, RING)], sems.at[s]))
        copies[-1].start()
    for c in copies:
        c.wait()
    upper = lax.broadcasted_iota(jnp.int32, (8, WIDTH), 0) < 4
    parts = 4
    depth = HALF // parts
    leave = []
    for part in range(parts):
        for l in range(part * depth, (part + 1) * depth):
            for h in range(2):
                a = held[2 * h, 8 * l:8 * l + 8, :]
                b = held[2 * h + 1, 8 * l:8 * l + 8, :]
                ready[l, 8 * h:8 * h + 8, :] = jnp.where(upper, a, pltpu.roll(b, 4, 0))
                ready[LAYERS - 1 - l, 8 * h:8 * h + 8, :] = jnp.where(upper, pltpu.roll(a, 4, 0), b)
        for i, low in enumerate((part * depth, LAYERS - (part + 1) * depth)):
            span = pl.ds(low, depth)
            leave.append(pltpu.make_async_copy(ready.at[span], out.at[span], out_sems.at[2 * part + i]))
            leave[-1].start()
    for c in leave:
        c.wait()


def shards(moisture, ancestors, adjacency, conductance, vertical, rainfall):
    ids = jnp.stack([lax.axis_index("tile"), lax.axis_index("dom")]).astype(jnp.int32)

    flat = moisture.reshape(LAYERS * GROUP, WIDTH)
    sent = pl.pallas_call(
        send_kernel,
        out_shape=shape((2 * GROUPS, LAYERS, WIDTH)),
        in_specs=[SMEM, SMEM, ANY],
        out_specs=ANY,
        scratch_shapes=[
            pltpu.VMEM((WIDTH // SPAN, LAYERS * GROUP, SPAN), F32),
            pltpu.VMEM((2 * GROUPS, LAYERS, WIDTH), F32),
            pltpu.SemaphoreType.DMA((WIDTH // SPAN,)),
            pltpu.SemaphoreType.DMA((GROUPS,)),
        ],
        compiler_params=params(12),
    )(ids, ancestors, flat)
    coeff = pl.pallas_call(
        coeff_kernel,
        out_shape=shape((MSG, SPAN)),
        in_specs=[SMEM, VMEM, VMEM, VMEM, ANY],
        out_specs=VMEM,
        compiler_params=params(8),
    )(ids, adjacency.T, conductance, vertical, sent)
    c_ring = [coeff] + [lax.ppermute(coeff, "tile", z_pairs(s)) for s in range(1, RING)]
    c_low, c_high = pl.pallas_call(
        edge_kernel,
        out_shape=[shape((2, MSG, SPAN))] * 2,
        in_specs=[SMEM] + [ANY] * RING,
        out_specs=[ANY] * 2,
        scratch_shapes=[pltpu.SemaphoreType.DMA((RING,))],
        compiler_params=params(4),
    )(ids, *c_ring)
    c_parts = [c_low, c_high, lax.ppermute(c_low, "tile", row_pairs(-1)), lax.ppermute(c_high, "tile", row_pairs(1))]
    got = lax.all_to_all(sent, "dom", split_axis=0, concat_axis=0, tiled=True)

    mine = pl.pallas_call(
        pack_kernel,
        out_shape=[shape((WIDTH // SPAN, ROWS + 8, SPAN))] * RING,
        in_specs=[SMEM, SMEM, VMEM, ANY],
        out_specs=[ANY] * RING,
        scratch_shapes=[
            pltpu.VMEM((2 * GROUPS, LAYERS, WIDTH), F32),
            pltpu.VMEM((RING, WIDTH // SPAN, ROWS + 8, SPAN), F32),
            pltpu.SMEM((GROUPS,), jnp.int32),
            pltpu.SemaphoreType.DMA,
            pltpu.SemaphoreType.DMA((RING,)),
        ],
        compiler_params=params(12),
    )(ids, ancestors, rainfall, got)
    ring = [mine[0]] + [lax.ppermute(mine[s], "tile", z_pairs(s)) for s in range(1, RING)]
    *c_parts, ring[0], ring[1], ring[2], ring[3] = lax.optimization_barrier((*c_parts, *ring))
    c_all = []
    for c in c_parts:
        c_all += [c, lax.ppermute(c, "dom", core_pairs())]
    state = (WIDTH // SPAN, ROWS + 8, SPAN)
    low, high = pl.pallas_call(
        edge_kernel,
        out_shape=[shape((2, *state)), shape((2, *state))],
        in_specs=[SMEM] + [ANY] * RING,
        out_specs=[ANY] * 2,
        scratch_shapes=[pltpu.SemaphoreType.DMA((RING,))],
        compiler_params=params(4),
    )(ids, *ring)
    side = [lax.ppermute(low, "tile", row_pairs(-1)), lax.ppermute(high, "tile", row_pairs(1))]

    coefs = pl.pallas_call(
        expand_kernel,
        out_shape=[shape((PAIRS, 2, 4 * SPAN, 2 * SPAN), BF16), shape((PAIRS, 6 * HALF + 8, 2 * SPAN))],
        in_specs=[SMEM] + [VMEM] * 8,
        out_specs=[VMEM] * 2,
        scratch_shapes=[pltpu.VMEM((PAIRS, LAYERS, 2 * SPAN), F32)],
        compiler_params=params(26),
    )(ids, *c_all)

    back = pl.pallas_call(
        step_kernel,
        out_shape=[shape((ROWS, WIDTH))] * RING,
        in_specs=[SMEM] + [VMEM] * 8,
        out_specs=[ANY] * RING,
        scratch_shapes=[pltpu.VMEM((2 * ROWS, (2 * PAIRS + 2) * SPAN), BF16)] * 2
        + [pltpu.VMEM((8, 2 * PAIRS * SPAN), F32)]
        + [pltpu.VMEM((ROWS, 2 * SPAN), F32)] * 4
        + [
            pltpu.VMEM((RING, ROWS, WIDTH), F32),
            pltpu.VMEM((PAIRS, 3 * HALF + 1, 8, 2 * SPAN), F32),
            pltpu.SemaphoreType.DMA((RING,)),
        ],
        compiler_params=params(46),
    )(ids, *ring, *side, *coefs)

    home = [back[0]] + [lax.ppermute(back[s], "tile", z_pairs(s)) for s in range(1, RING)]
    return pl.pallas_call(
        join_kernel,
        out_shape=shape((LAYERS, GROUP, WIDTH)),
        in_specs=[SMEM] + [ANY] * RING,
        out_specs=ANY,
        scratch_shapes=[
            pltpu.VMEM((RING, ROWS, WIDTH), F32),
            pltpu.VMEM((LAYERS, GROUP, WIDTH), F32),
            pltpu.SemaphoreType.DMA((RING,)),
            pltpu.SemaphoreType.DMA((8,)),
        ],
        compiler_params=params(14),
    )(ids, *home)


def solution(mesh):
    in_specs = (
        P(None, "dom", "tile"),
        P(),
        P(),
        P("tile", None, None, None),
        P(None, "tile"),
        P("dom", "tile"),
    )
    out_specs = P(None, "dom", "tile")
    return jax.shard_map(shards, mesh=mesh, in_specs=in_specs, out_specs=out_specs, check_vma=False)
```
